128 devices in a mesh: row: 8 (over y, z_hi), col: 16 (over x, z_lo, core).
Axes of the slice: x: 4, y: 4, z: 4 (z_hi: 2, z_lo: 2; z = z_hi * 2 + z_lo), core: 2. Of those that a mesh axis runs over, the one named last changes fastest.
Arguments:
- tokens: bfloat16 [16448, 1024], P('row', 'col'), may hold values from -6 to 6
- qkv_weight: bfloat16 [1024, 3072], P('col', 'row'), may hold values from -2 to 2
- persistent: bfloat16 [16, 2, 1024], P(None, None, 'row'), may hold values from -6 to 6
- cache_pages: bfloat16 [1024, 256, 2, 1024], P('col', None, None, 'row'), may hold values from -48 to 48
- page_table: int32 [64, 16], P('col'), may hold values from 0 to 63, as said below
- cache_len: int32 [64], P('col'), may hold values from 1 to 4096, as said below
- destination: int32 [16], P('col'), may hold values from 0 to 15, each once
- memory_in: float32 [16, 8, 128, 128], P('col', 'row'), may hold values from -6 to 6
- momentum_in: float32 [16, 8, 128, 128], P('col', 'row'), may hold values from -3 to 3
- forget_rate: float32 [16, 8, 16], P('col', 'row'), may hold values from 0.02 to 0.5
- keep_rate: float32 [16, 8, 16], P('col', 'row'), may hold values from 0.3 to 0.95
- learn_rate: float32 [16, 8, 16], P('col', 'row'), may hold values from 0.05 to 1
- decode_memory: float32 [64, 8, 128, 128], P('col', 'row'), may hold values from -6 to 6
Outputs:
- heads_out: bfloat16 [16448, 1024], P('col', 'row')
- memory_out: float32 [16, 8, 128, 128], P('col', 'row')
- momentum_out: float32 [16, 8, 128, 128], P('col', 'row')
The draws below stay inside these ranges and needn't reach their ends.
Inputs may be any that keep to these rules, and one draw needn't show every extreme that they name: `page_table`: the 4 decode requests of one index of col together name every page of that index's pool once. `cache_len`: some request has exactly 4096. `destination`: each request block once.
All inputs are finite; a program needn't handle non-finite values.
Results may differ from the reference program's by a relative error of at most 0.012.
The reference program's roundings to bfloat16 on the way count: a program that leaves them out, or rounds other values in their place, can miss the bound.
Values may be sent and summed in bfloat16 or wider, within the bound.
No kernel may reach another device: no remote copies, remote signals or barrier semaphores. Data moves between devices by JAX's collectives and lax.ppermute only.
A program may use at most 128 MiB of HBM per device.

```python
import math
import jax
import jax.numpy as jnp
from jax import lax

D = 1024
H = 8
HD = 128
PERS = 16
MCH = 64
PCH = 1024
DEC_DEV = 4
CACHE = 4096
PAGE = 256
NCH = 16
PREFILL = 16
DECODE = 64
TOKENS = 16448
POOLS = 1024
N_COL = 16


def draw_qkv_weight(key, part):
    values = jnp.clip(jax.random.normal(jax.random.fold_in(key, 31), (D, 3 * D), jnp.float32), -6.0, 6.0) * D ** (-0.5)
    return jnp.clip(values, -2.0, 2.0).astype(jnp.bfloat16)


def draw_cache_pages(key, part):
    values = jnp.clip(jax.random.normal(jax.random.fold_in(key, 53), (POOLS, PAGE, 2, D), jnp.float32), -6.0, 6.0)
    return values.astype(jnp.bfloat16)


def draw_page_table(key, part):
    blocks = DECODE // DEC_DEV
    key_list = jax.random.split(key, blocks)
    orders = jax.vmap(lambda block_key: jax.random.permutation(block_key, DEC_DEV * (CACHE // PAGE)))(key_list)
    return orders.reshape(DECODE, CACHE // PAGE).astype(jnp.int32)


def draw_cache_len(key, part):
    first_key, second_key = jax.random.split(key)
    lengths = jax.random.randint(first_key, (DECODE,), 1, CACHE + 1)
    longest = jax.random.randint(second_key, (), 0, DECODE)
    return jnp.where(jnp.arange(DECODE) == longest, CACHE, lengths).astype(jnp.int32)


def block_levels(own_key, dims, cuts, least, top_value):
    gain = 1.0
    for axis_at, parts in cuts:
        draws = jax.random.uniform(jax.random.fold_in(jax.random.fold_in(own_key, 6), axis_at), (parts,), jnp.float32, least / len(cuts), top_value / len(cuts))
        gain = gain * jnp.repeat(jnp.exp(draws), dims[axis_at] // parts).reshape((-1,) + (1,) * (len(dims) - 1 - axis_at))
    return gain


def normal_values(rng, dims, spread, bound, cuts=(), kind=jnp.bfloat16):
    level = block_levels(rng, dims, cuts, -0.22, 0.18) if cuts else 1.0
    result = jax.random.normal(rng, dims, jnp.float32) * spread * level
    return jnp.minimum(jnp.maximum(result, -bound), bound).astype(kind)


def setup_inputs(seed: int = 0) -> dict:
    arg_keys = jax.random.split(jax.random.key(seed), 14)
    return {
        "tokens": normal_values(arg_keys[0], (TOKENS, D), 1.0, 6.0, ((0, 8), (1, 16))),
        "qkv_weight": draw_qkv_weight(jax.random.fold_in(arg_keys[13], 71), 0),
        "persistent": normal_values(arg_keys[2], (PERS, 2, D), 1.0, 6.0, ((2, 8),)),
        "cache_pages": draw_cache_pages(jax.random.fold_in(arg_keys[13], 71), 0),
        "page_table": draw_page_table(jax.random.fold_in(arg_keys[13], 71), 0),
        "cache_len": draw_cache_len(jax.random.fold_in(arg_keys[13], 71), 0),
        "destination": jax.random.permutation(arg_keys[6], PREFILL).astype(jnp.int32),
        "memory_in": normal_values(arg_keys[7], (PREFILL, H, HD, HD), 1.0, 6.0, ((0, 16), (1, 8)), jnp.float32),
        "momentum_in": normal_values(arg_keys[8], (PREFILL, H, HD, HD), 0.5, 3.0, ((0, 16), (1, 8)), jnp.float32),
        "forget_rate": jnp.clip(0.02 + 0.48 * jax.random.uniform(arg_keys[9], (PREFILL, H, NCH), jnp.float32) ** block_levels(arg_keys[9], (PREFILL, H, NCH), ((0, 16), (1, 8)), -0.2, 0.2), 0.02, 0.5),
        "keep_rate": jnp.clip(0.3 + 0.65 * jax.random.uniform(arg_keys[10], (PREFILL, H, NCH), jnp.float32) ** block_levels(arg_keys[10], (PREFILL, H, NCH), ((0, 16), (1, 8)), -0.2, 0.2), 0.3, 0.95),
        "learn_rate": jnp.clip(jnp.exp(math.log(1.0) - 2.9957323 * jax.random.uniform(arg_keys[11], (PREFILL, H, NCH), jnp.float32) ** block_levels(arg_keys[11], (PREFILL, H, NCH), ((0, 16), (1, 8)), -0.2, 0.2)), 0.05, 1.0),
        "decode_memory": normal_values(arg_keys[12], (DECODE, H, HD, HD), 1.0, 6.0, ((0, 16), (1, 8)), jnp.float32),
    }


epsilon = 1e-06
highest = lax.Precision.HIGHEST

def unit_rows(values):
    return values / jnp.sqrt(lax.optimization_barrier(jnp.sum(values * values, axis=-1, keepdims=True)) + epsilon)

def memory_spans(query_unit, key_unit, value_rows, memory, momentum, forget_rate, keep_rate, learn_rate):

    def advance(carry, inputs):
        memory_now, momentum_now = carry
        query_now, key_now, value_now, forget_now, keep_now, learn_now = inputs
        readout = jnp.dot(query_now, memory_now, precision=highest)
        errors = jnp.dot(key_now, memory_now, precision=highest) - value_now
        gradient = jnp.dot(key_now.T, errors, precision=highest) * (2.0 / MCH)
        momentum_now = keep_now * momentum_now - learn_now * gradient
        memory_now = (1.0 - forget_now) * memory_now + momentum_now
        return ((memory_now, momentum_now), readout)
    (memory, momentum), readouts = lax.scan(advance, (memory, momentum), (query_unit, key_unit, value_rows, forget_rate, keep_rate, learn_rate))
    return (readouts, memory, momentum)

def window_attention(query_rows, key_rows, value_rows, persist_key, persist_value):
    scale_factor = query_rows.shape[-1] ** (-0.5)
    inner_score = jnp.einsum('nqd,nkd->nqk', query_rows.astype(jnp.float32), key_rows.astype(jnp.float32)) * scale_factor
    length_q = query_rows.shape[1]
    causal = jnp.arange(length_q)[:, None] >= jnp.arange(length_q)[None, :]
    inner_score = jnp.where(causal[None], inner_score, -jnp.inf)
    outer_score = jnp.einsum('nqd,pd->nqp', query_rows.astype(jnp.float32), persist_key.astype(jnp.float32)) * scale_factor
    highest_score = jnp.maximum(lax.optimization_barrier(jnp.max(inner_score, axis=-1)), lax.optimization_barrier(jnp.max(outer_score, axis=-1)))[..., None]
    inner_exp = jnp.exp(inner_score - highest_score)
    outer_exp = jnp.exp(outer_score - highest_score)
    totals = lax.optimization_barrier(jnp.sum(inner_exp, axis=-1, keepdims=True)) + lax.optimization_barrier(jnp.sum(outer_exp, axis=-1, keepdims=True))
    inner_weight = (inner_exp / totals).astype(jnp.bfloat16)
    outer_weight = (outer_exp / totals).astype(jnp.bfloat16)
    attended = jnp.einsum('nqk,nkd->nqd', inner_weight.astype(jnp.float32), value_rows.astype(jnp.float32))
    return attended + jnp.einsum('nqp,pd->nqd', outer_weight.astype(jnp.float32), persist_value.astype(jnp.float32))

def prefill_head(token_block, persist_key, persist_value, memory, momentum, forget_rate, keep_rate, learn_rate):
    spans = token_block.shape[0] // MCH
    query_rows = token_block[:, 0].reshape(spans, MCH, -1)
    key_rows = token_block[:, 1].reshape(spans, MCH, -1)
    value_rows = token_block[:, 2].reshape(spans, MCH, -1)
    readouts, memory, momentum = memory_spans(unit_rows(query_rows.astype(jnp.float32)), unit_rows(key_rows.astype(jnp.float32)), value_rows.astype(jnp.float32), memory, momentum, forget_rate, keep_rate, learn_rate)
    attended = window_attention(query_rows, key_rows, value_rows, persist_key, persist_value)
    return ((attended + readouts).reshape(-1, token_block.shape[-1]).astype(jnp.bfloat16), memory, momentum)

def decode_head(row_block, cache_block, persist_key, persist_value, memory_now, length_now):
    query_row = row_block[0].astype(jnp.float32)
    key_row = row_block[1].astype(jnp.float32)
    value_row = row_block[2].astype(jnp.float32)
    scale_factor = row_block.shape[-1] ** (-0.5)
    cache_score = jnp.dot(cache_block[:, 0].astype(jnp.float32), query_row) * scale_factor
    live_mask = jnp.arange(cache_block.shape[0]) < length_now
    cache_score = jnp.where(live_mask, cache_score, -jnp.inf)
    own_score = jnp.sum(query_row * key_row) * scale_factor
    persist_score = jnp.dot(persist_key.astype(jnp.float32), query_row) * scale_factor
    highest_score = jnp.maximum(jnp.maximum(jnp.max(cache_score), own_score), jnp.max(persist_score))
    cache_exp = jnp.exp(cache_score - highest_score)
    own_exp = jnp.exp(own_score - highest_score)
    persist_exp = jnp.exp(persist_score - highest_score)
    totals = jnp.sum(cache_exp) + own_exp + jnp.sum(persist_exp)
    cache_weight = (cache_exp / totals).astype(jnp.bfloat16)
    own_weight = (own_exp / totals).astype(jnp.bfloat16)
    persist_weight = (persist_exp / totals).astype(jnp.bfloat16)
    attended = jnp.dot(cache_weight.astype(jnp.float32), cache_block[:, 1].astype(jnp.float32))
    attended = attended + own_weight.astype(jnp.float32) * value_row
    attended = attended + jnp.dot(persist_weight.astype(jnp.float32), persist_value.astype(jnp.float32))
    readout = jnp.dot(unit_rows(query_row), memory_now, precision=highest)
    return (attended + readout).astype(jnp.bfloat16)

def reference(tokens, qkv_weight, persistent, cache_pages, page_table, cache_len, destination, memory_in, momentum_in, forget_rate, keep_rate, learn_rate, decode_memory):
    block_rows = PCH + DEC_DEV
    projected = jnp.dot(tokens, qkv_weight, preferred_element_type=jnp.float32).astype(jnp.bfloat16)
    projected = projected.reshape(N_COL, block_rows, H, 3, HD)
    persist = persistent.reshape(PERS, 2, H, HD)
    memory_all = jnp.zeros_like(memory_in).at[destination].set(memory_in)
    momentum_all = jnp.zeros_like(momentum_in).at[destination].set(momentum_in)
    head_map = jax.vmap(prefill_head, in_axes=(1, 1, 1, 0, 0, 0, 0, 0), out_axes=(1, 0, 0))

    def one_request(inputs):
        return head_map(inputs[0], persist[:, 0], persist[:, 1], inputs[1], inputs[2], inputs[3], inputs[4], inputs[5])
    prefill_out, memory_out, momentum_out = lax.map(one_request, (projected[:, :PCH], memory_all, momentum_all, forget_rate, keep_rate, learn_rate))
    decode_rows = projected[:, PCH:].reshape(N_COL * DEC_DEV, H, 3, HD)
    pool_dev = DEC_DEV * (CACHE // PAGE)
    owners = jnp.arange(N_COL * DEC_DEV, dtype=jnp.int32) // DEC_DEV
    head_decode = jax.vmap(decode_head, in_axes=(0, 2, 1, 1, 0, None))

    def one_decode(inputs):
        row_block, table_row, owner, length_now, memory_now = inputs
        cache_block = cache_pages[(owner * pool_dev + table_row).astype(jnp.int32)].reshape(CACHE, 2, H, HD)
        return head_decode(row_block, cache_block, persist[:, 0], persist[:, 1], memory_now, length_now)
    decode_out = lax.map(one_decode, (decode_rows, page_table, owners, cache_len, decode_memory))
    decode_out = decode_out.reshape(N_COL, DEC_DEV, H, HD)
    heads_out = jnp.concatenate([prefill_out, decode_out], axis=1).reshape(N_COL * block_rows, H * HD)
    return (heads_out, memory_out, momentum_out)
```

```python
import jax
import jax.numpy as jnp
from jax import lax
from jax.experimental import pallas as pl
from jax.experimental.pallas import tpu as pltpu
from jax.sharding import PartitionSpec as P

HD = 128
PERS = 16
MCH = 64
PCH = 1024
DEC_DEV = 4
CACHE = 4096
PAGE = 256
PAGES = CACHE // PAGE
ROWS = PCH + DEC_DEV
PADDED = PCH + 16

F32 = jnp.float32
BF16 = jnp.bfloat16
EPSILON = 1e-6
SCALE = HD**-0.5


def device_at(x, y, z_hi, z_lo, core):
    return (2 * y + z_hi) * 16 + 4 * x + 2 * z_lo + core


def moves(target):
    pairs = []
    for x in range(4):
        for y in range(4):
            for z_hi in range(2):
                for z_lo in range(2):
                    for core in range(2):
                        here = (x, y, z_hi, z_lo, core)
                        pairs.append((device_at(*here), device_at(*target(*here))))
    return pairs


def permute(values, target):
    return lax.ppermute(values, ("row", "col"), moves(target))


def dot_f32(left, right):
    return lax.dot_general(left, right, (((1,), (0,)), ((), ())), preferred_element_type=F32)


def dot_rows(left, right):
    return lax.dot_general(left, right, (((1,), (1,)), ((), ())), preferred_element_type=F32)


def dot_turned(left, right):
    return lax.dot_general(left, right, (((0,), (0,)), ((), ())), preferred_element_type=F32)


def two_parts(values):
    high = values.astype(BF16)
    return jnp.concatenate([high, (values - high.astype(F32)).astype(BF16)], axis=0)


def inverse_norm(rows):
    wide = rows.astype(F32)
    return lax.rsqrt(jnp.sum(wide * wide, axis=-1, keepdims=True) + EPSILON)


def layer_kernel(
    table_ref,
    length_ref,
    forget_ref,
    keep_ref,
    learn_ref,
    token_ref,
    weight_ref,
    persist_key_ref,
    persist_value_ref,
    state_ref,
    decode_memory_ref,
    page_ref,
    out_ref,
    memory_ref,
    momentum_ref,
    projected,
    cache,
    score,
    arrival,
):
    for request in range(DEC_DEV):
        for place in range(PAGES):
            pltpu.make_async_copy(
                page_ref.at[table_ref[request * PAGES + place]],
                cache.at[request, pl.ds(place * 2 * PAGE, 2 * PAGE)],
                arrival.at[request],
            ).start()

    total = None
    for chunk in range(4):
        rows = jnp.concatenate([token_ref[2 * chunk], token_ref[2 * chunk + 1]], axis=1)
        part = dot_f32(rows, weight_ref[256 * chunk : 256 * chunk + 256, :])
        total = part if total is None else total + part
    projected[...] = total.astype(BF16)

    persist_key = persist_key_ref[...]
    persist_value = persist_value_ref[...]
    blank = jnp.zeros((HD - MCH - PERS, HD), BF16)
    row_at = lax.broadcasted_iota(jnp.int32, (MCH, HD), 0)
    column_at = lax.broadcasted_iota(jnp.int32, (MCH, HD), 1)
    visible = (column_at <= row_at) | ((column_at >= MCH) & (column_at < MCH + PERS))

    memory = jnp.concatenate([state_ref[s, 0:8, :] for s in range(16)], axis=0)
    momentum = jnp.concatenate([state_ref[s, 8:16, :] for s in range(16)], axis=0)
    for block in range(PCH // MCH):
        here = slice(block * MCH, block * MCH + MCH)
        query = projected[here, 0:HD]
        key = projected[here, HD : 2 * HD]
        value = projected[here, 2 * HD : 3 * HD]
        query_scale = inverse_norm(query)
        key_scale = inverse_norm(key)
        left = jnp.concatenate(
            [jnp.concatenate([query, query], axis=1), jnp.concatenate([key, key], axis=1)], axis=0
        )
        reads = dot_f32(left, two_parts(memory))
        errors = reads[MCH:] * key_scale - value.astype(F32)
        errors = errors * (key_scale * (2.0 / MCH))
        gradient = dot_turned(jnp.concatenate([key, key], axis=0), two_parts(errors))
        momentum = keep_ref[block] * momentum - learn_ref[block] * gradient
        memory = (1.0 - forget_ref[block]) * memory + momentum

        keys = jnp.concatenate([key, persist_key, blank], axis=0)
        values = jnp.concatenate([value, persist_value, blank], axis=0)
        scores = jnp.where(visible, dot_rows(query, keys) * SCALE, -jnp.inf)
        powers = jnp.exp(scores - jnp.max(scores, axis=-1, keepdims=True))
        weights = (powers / jnp.sum(powers, axis=-1, keepdims=True)).astype(BF16)
        out_ref[here, :] = (dot_f32(weights, values) + reads[:MCH] * query_scale).astype(BF16)
    memory_ref[...] = memory
    momentum_ref[...] = momentum

    query = projected[PCH:PADDED, 0:HD]
    key = projected[PCH:PADDED, HD : 2 * HD]
    value = projected[PCH:PADDED, 2 * HD : 3 * HD]
    row = lax.broadcasted_iota(jnp.int32, (16, 1), 0)
    length = jnp.zeros((16, 1), jnp.int32)
    for request in range(DEC_DEV):
        pltpu.make_async_copy(cache.at[request], cache.at[request], arrival.at[request]).wait()
        length = jnp.where(row == request, length_ref[request], length)
    for place in range(PAGES):
        span = slice(place * 2 * PAGE, place * 2 * PAGE + 2 * PAGE)
        found = dot_rows(query, cache[0, span, :])
        for request in range(1, DEC_DEV):
            found = jnp.where(row == request, dot_rows(query, cache[request, span, :]), found)
        column = lax.broadcasted_iota(jnp.int32, (16, 2 * PAGE), 1)
        live = ((column & 1) == 0) & ((column >> 1) + place * PAGE < length)
        score[:, span] = jnp.where(live, found * SCALE, -jnp.inf)
    own_score = jnp.sum(query.astype(F32) * key.astype(F32), axis=-1, keepdims=True) * SCALE
    persist_score = dot_rows(query, persist_key) * SCALE
    cache_score = score[...]
    largest = jnp.maximum(
        jnp.maximum(jnp.max(cache_score, axis=-1, keepdims=True), own_score),
        jnp.max(persist_score, axis=-1, keepdims=True),
    )
    cache_power = jnp.exp(cache_score - largest)
    own_power = jnp.exp(own_score - largest)
    persist_power = jnp.exp(persist_score - largest)
    totals = (
        jnp.sum(cache_power, axis=-1, keepdims=True)
        + own_power
        + jnp.sum(persist_power, axis=-1, keepdims=True)
    )
    share = 1.0 / totals
    cache_weight = pltpu.roll(cache_power * share, 1, 1).astype(BF16)
    attended = jnp.zeros((16, HD), F32)
    for request in range(DEC_DEV):
        attended = jnp.where(row == request, dot_f32(cache_weight, cache[request]), attended)
    own_weight = (own_power * share).astype(BF16).astype(F32)
    attended = attended + own_weight * value.astype(F32)
    attended = attended + dot_f32((persist_power * share).astype(BF16), persist_value)
    twice = jnp.concatenate([query, query], axis=1)
    readout = jnp.zeros((16, HD), F32)
    for request in range(DEC_DEV):
        readout = jnp.where(row == request, dot_f32(twice, two_parts(decode_memory_ref[request])), readout)
    result = (attended + readout * inverse_norm(query)).astype(BF16)
    out_ref[PCH:ROWS, :] = result[:DEC_DEV]


def layer(table, length, forget, keep, learn, chunks, weight, persist, state, decode_memory, pages):
    in_smem = pl.BlockSpec(memory_space=pltpu.SMEM)
    in_vmem = pl.BlockSpec(memory_space=pltpu.VMEM)
    return pl.pallas_call(
        layer_kernel,
        out_shape=(
            jax.ShapeDtypeStruct((ROWS, HD), BF16),
            jax.ShapeDtypeStruct((HD, HD), F32),
            jax.ShapeDtypeStruct((HD, HD), F32),
        ),
        in_specs=[in_smem] * 5 + [in_vmem] * 6 + [pl.BlockSpec(memory_space=pl.ANY)],
        out_specs=(in_vmem, in_vmem, in_vmem),
        scratch_shapes=[
            pltpu.VMEM((PADDED, 3 * HD), BF16),
            pltpu.VMEM((DEC_DEV, 2 * CACHE, HD), BF16),
            pltpu.VMEM((16, 2 * CACHE), F32),
            pltpu.SemaphoreType.DMA((DEC_DEV,)),
        ],
        compiler_params=pltpu.CompilerParams(vmem_limit_bytes=40 * 2**20),
    )(
        table.reshape(-1),
        length,
        forget.reshape(-1),
        keep.reshape(-1),
        learn.reshape(-1),
        chunks,
        weight,
        persist[:, 0],
        persist[:, 1],
        state,
        decode_memory.reshape(DEC_DEV, HD, HD),
        pages.reshape(DEC_DEV * PAGES, 2 * PAGE, HD),
    )


def route_states(memory_in, momentum_in, destination):
    slots = 16
    mark = jnp.broadcast_to(destination.astype(F32).reshape(1, 1, 1), (slots, 8, HD))
    pieces = jnp.concatenate(
        [memory_in.reshape(slots, 8, HD), momentum_in.reshape(slots, 8, HD), mark], axis=1
    )
    spread = lax.all_to_all(pieces, "col", split_axis=0, concat_axis=0, tiled=True)
    target = spread[:, 16, 0].astype(jnp.int32)
    chosen = target[None, :] == jnp.arange(slots, dtype=jnp.int32)[:, None]
    ordered = jnp.sum(
        jnp.where(chosen[:, :, None, None], spread[None, :, :16, :], 0.0), axis=1
    )
    return lax.all_to_all(ordered, "col", split_axis=0, concat_axis=0, tiled=True)


def shards(
    tokens,
    qkv_weight,
    persistent,
    cache_pages,
    page_table,
    cache_len,
    destination,
    memory_in,
    momentum_in,
    forget_rate,
    keep_rate,
    learn_rate,
    decode_memory,
):
    core = lax.axis_index("col") % 2
    halves = tokens.reshape(2, ROWS, tokens.shape[1])
    kept = lax.dynamic_index_in_dim(halves, core, 0, keepdims=False)
    sent = lax.dynamic_index_in_dim(halves, 1 - core, 0, keepdims=False)
    came = permute(sent, lambda x, y, z_hi, z_lo, core: (x, y, z_hi, z_lo, 1 - core))
    own = jnp.concatenate(
        [jnp.where(core == 0, kept, came), jnp.where(core == 0, came, kept)], axis=1
    )
    own = jnp.pad(own, ((0, PADDED - ROWS), (0, 0)))
    turned = permute(own, lambda x, y, z_hi, z_lo, core: (y, x, z_lo, z_hi, core))
    chunks = lax.all_to_all(
        jnp.broadcast_to(turned[None], (8, PADDED, HD)),
        "row",
        split_axis=0,
        concat_axis=0,
        tiled=True,
    )
    weight = lax.all_gather(qkv_weight, "col", axis=0, tiled=True)
    state = route_states(memory_in, momentum_in, destination)
    heads_out, memory, momentum = layer(
        page_table,
        cache_len,
        forget_rate,
        keep_rate,
        learn_rate,
        chunks,
        weight,
        persistent,
        state,
        decode_memory,
        cache_pages,
    )
    return heads_out, memory[None, None], momentum[None, None]


def solution(mesh):
    placed = (
        P("row", "col"),
        P("col", "row"),
        P(None, None, "row"),
        P("col", None, None, "row"),
        P("col", None),
        P("col"),
        P("col"),
        P("col", "row", None, None),
        P("col", "row", None, None),
        P("col", "row", None),
        P("col", "row", None),
        P("col", "row", None),
        P("col", "row", None, None),
    )
    return jax.shard_map(
        shards,
        mesh=mesh,
        in_specs=placed,
        out_specs=(P("col", "row"), P("col", "row", None, None), P("col", "row", None, None)),
        check_vma=False,
    )
```

```python
import jax
import jax.numpy as jnp
from jax import lax
from jax.experimental import pallas as pl
from jax.experimental.pallas import tpu as pltpu
from jax.sharding import PartitionSpec as P

HD = 128
PERS = 16
MCH = 64
PCH = 1024
DEC_DEV = 4
CACHE = 4096
PAGE = 256
PAGES = CACHE // PAGE
ROWS = PCH + DEC_DEV
PADDED = PCH + 16

F32 = jnp.float32
BF16 = jnp.bfloat16
EPSILON = 1e-6
SCALE = HD**-0.5


def device_at(x, y, z_hi, z_lo, core):
    return (2 * y + z_hi) * 16 + 4 * x + 2 * z_lo + core


def moves(target):
    pairs = []
    for x in range(4):
        for y in range(4):
            for z_hi in range(2):
                for z_lo in range(2):
                    for core in range(2):
                        here = (x, y, z_hi, z_lo, core)
                        pairs.append((device_at(*here), device_at(*target(*here))))
    return pairs


def permute(values, target):
    return lax.ppermute(values, ("row", "col"), moves(target))


def dot_f32(left, right):
    return lax.dot_general(left, right, (((1,), (0,)), ((), ())), preferred_element_type=F32)


def dot_rows(left, right):
    return lax.dot_general(left, right, (((1,), (1,)), ((), ())), preferred_element_type=F32)


def dot_turned(left, right):
    return lax.dot_general(left, right, (((0,), (0,)), ((), ())), preferred_element_type=F32)


def two_parts(values):
    high = values.astype(BF16)
    return jnp.concatenate([high, (values - high.astype(F32)).astype(BF16)], axis=0)


def inverse_norm(rows):
    wide = rows.astype(F32)
    return lax.rsqrt(jnp.sum(wide * wide, axis=-1, keepdims=True) + EPSILON)


HALF = PCH // 2
EXTRA = PADDED - PCH


def project(token_refs, weight_ref):
    total = None
    for step, token_ref in enumerate(token_refs):
        part = dot_f32(token_ref[...], weight_ref[256 * step : 256 * step + 256, :])
        total = part if total is None else total + part
    return total.astype(BF16)


def prefill(
    first, projected, persist_key, persist_value, memory, momentum, rates, out_ref, out_at
):
    forget_ref, keep_ref, learn_ref = rates
    blank = jnp.zeros((HD - MCH - PERS, HD), BF16)
    row_at = lax.broadcasted_iota(jnp.int32, (MCH, HD), 0)
    column_at = lax.broadcasted_iota(jnp.int32, (MCH, HD), 1)
    visible = (column_at <= row_at) | ((column_at >= MCH) & (column_at < MCH + PERS))
    for step in range(HALF // MCH):
        block = first + step
        here = slice(step * MCH, step * MCH + MCH)
        query = projected[here, 0:HD]
        key = projected[here, HD : 2 * HD]
        value = projected[here, 2 * HD : 3 * HD]
        query_scale = inverse_norm(query)
        key_scale = inverse_norm(key)
        left = jnp.concatenate(
            [jnp.concatenate([query, query], axis=1), jnp.concatenate([key, key], axis=1)], axis=0
        )
        reads = dot_f32(left, two_parts(memory))
        errors = reads[MCH:] * key_scale - value.astype(F32)
        errors = errors * (key_scale * (2.0 / MCH))
        gradient = dot_turned(jnp.concatenate([key, key], axis=0), two_parts(errors))
        momentum = keep_ref[block] * momentum - learn_ref[block] * gradient
        memory = (1.0 - forget_ref[block]) * memory + momentum

        keys = jnp.concatenate([key, persist_key, blank], axis=0)
        values = jnp.concatenate([value, persist_value, blank], axis=0)
        scores = jnp.where(visible, dot_rows(query, keys) * SCALE, -jnp.inf)
        powers = jnp.exp(scores - jnp.max(scores, axis=-1, keepdims=True))
        weights = (powers / jnp.sum(powers, axis=-1, keepdims=True)).astype(BF16)
        result = dot_f32(weights, values) + reads[:MCH] * query_scale
        out_ref[out_at + step * MCH : out_at + step * MCH + MCH, :] = result.astype(BF16)
    return memory, momentum


def decode(
    length_ref, projected, persist_key, persist_value, decode_memory_ref, cache, score, arrival
):
    query = projected[HALF : HALF + EXTRA, 0:HD]
    key = projected[HALF : HALF + EXTRA, HD : 2 * HD]
    value = projected[HALF : HALF + EXTRA, 2 * HD : 3 * HD]
    row = lax.broadcasted_iota(jnp.int32, (EXTRA, 1), 0)
    length = jnp.zeros((EXTRA, 1), jnp.int32)
    for request in range(DEC_DEV):
        pltpu.make_async_copy(cache.at[request], cache.at[request], arrival.at[request]).wait()
        length = jnp.where(row == request, length_ref[request], length)
    for place in range(PAGES):
        span = slice(place * 2 * PAGE, place * 2 * PAGE + 2 * PAGE)
        found = dot_rows(query, cache[0, span, :])
        for request in range(1, DEC_DEV):
            found = jnp.where(row == request, dot_rows(query, cache[request, span, :]), found)
        column = lax.broadcasted_iota(jnp.int32, (EXTRA, 2 * PAGE), 1)
        live = ((column & 1) == 0) & ((column >> 1) + place * PAGE < length)
        score[:, span] = jnp.where(live, found * SCALE, -jnp.inf)
    own_score = jnp.sum(query.astype(F32) * key.astype(F32), axis=-1, keepdims=True) * SCALE
    persist_score = dot_rows(query, persist_key) * SCALE
    cache_score = score[...]
    largest = jnp.maximum(
        jnp.maximum(jnp.max(cache_score, axis=-1, keepdims=True), own_score),
        jnp.max(persist_score, axis=-1, keepdims=True),
    )
    cache_power = jnp.exp(cache_score - largest)
    own_power = jnp.exp(own_score - largest)
    persist_power = jnp.exp(persist_score - largest)
    totals = (
        jnp.sum(cache_power, axis=-1, keepdims=True)
        + own_power
        + jnp.sum(persist_power, axis=-1, keepdims=True)
    )
    share = 1.0 / totals
    cache_weight = pltpu.roll(cache_power * share, 1, 1).astype(BF16)
    attended = jnp.zeros((EXTRA, HD), F32)
    for request in range(DEC_DEV):
        attended = jnp.where(row == request, dot_f32(cache_weight, cache[request]), attended)
    own_weight = (own_power * share).astype(BF16).astype(F32)
    attended = attended + own_weight * value.astype(F32)
    attended = attended + dot_f32((persist_power * share).astype(BF16), persist_value)
    twice = jnp.concatenate([query, query], axis=1)
    readout = jnp.zeros((EXTRA, HD), F32)
    for request in range(DEC_DEV):
        read = dot_f32(twice, two_parts(decode_memory_ref[request]))
        readout = jnp.where(row == request, read, readout)
    return (attended + readout * inverse_norm(query)).astype(BF16)


def first_kernel(
    table_ref,
    length_ref,
    forget_ref,
    keep_ref,
    learn_ref,
    token_0_ref,
    token_1_ref,
    token_2_ref,
    token_3_ref,
    weight_ref,
    persist_key_ref,
    persist_value_ref,
    state_ref,
    decode_memory_ref,
    page_ref,
    out_ref,
    tail_ref,
    memory_ref,
    momentum_ref,
    projected,
    cache,
    score,
    arrival,
):
    for request in range(DEC_DEV):
        for place in range(PAGES):
            pltpu.make_async_copy(
                page_ref.at[table_ref[request * PAGES + place]],
                cache.at[request, pl.ds(place * 2 * PAGE, 2 * PAGE)],
                arrival.at[request],
            ).start()
    projected[...] = project((token_0_ref, token_1_ref, token_2_ref, token_3_ref), weight_ref)
    memory = jnp.concatenate([state_ref[s, 0:8, :] for s in range(16)], axis=0)
    momentum = jnp.concatenate([state_ref[s, 8:16, :] for s in range(16)], axis=0)
    persist_key, persist_value = persist_key_ref[...], persist_value_ref[...]
    rates = (forget_ref, keep_ref, learn_ref)
    memory, momentum = prefill(
        0, projected, persist_key, persist_value, memory, momentum, rates, out_ref, 0
    )
    memory_ref[...] = memory
    momentum_ref[...] = momentum
    tail_ref[...] = decode(
        length_ref, projected, persist_key, persist_value, decode_memory_ref, cache, score, arrival
    )


def second_kernel(
    forget_ref,
    keep_ref,
    learn_ref,
    token_0_ref,
    token_1_ref,
    token_2_ref,
    token_3_ref,
    weight_ref,
    persist_key_ref,
    persist_value_ref,
    memory_in_ref,
    momentum_in_ref,
    first_ref,
    tail_ref,
    out_ref,
    memory_ref,
    momentum_ref,
    projected,
):
    projected[...] = project((token_0_ref, token_1_ref, token_2_ref, token_3_ref), weight_ref)
    memory, momentum = prefill(
        HALF // MCH,
        projected,
        persist_key_ref[...],
        persist_value_ref[...],
        memory_in_ref[...],
        momentum_in_ref[...],
        (forget_ref, keep_ref, learn_ref),
        out_ref,
        HALF,
    )
    memory_ref[...] = memory
    momentum_ref[...] = momentum
    out_ref[0:HALF, :] = first_ref[...]
    out_ref[PCH:ROWS, :] = tail_ref[0:DEC_DEV, :]


IN_SMEM = pl.BlockSpec(memory_space=pltpu.SMEM)
IN_VMEM = pl.BlockSpec(memory_space=pltpu.VMEM)


def first_part(table, length, rates, chunks, weight, keys, values, state, decode_memory, pages):
    return pl.pallas_call(
        first_kernel,
        out_shape=(
            jax.ShapeDtypeStruct((HALF, HD), BF16),
            jax.ShapeDtypeStruct((EXTRA, HD), BF16),
            jax.ShapeDtypeStruct((HD, HD), F32),
            jax.ShapeDtypeStruct((HD, HD), F32),
        ),
        in_specs=[IN_SMEM] * 5 + [IN_VMEM] * 9 + [pl.BlockSpec(memory_space=pltpu.HBM)],
        out_specs=(IN_VMEM,) * 4,
        scratch_shapes=[
            pltpu.VMEM((HALF + EXTRA, 3 * HD), BF16),
            pltpu.VMEM((DEC_DEV, 2 * CACHE, HD), BF16),
            pltpu.VMEM((EXTRA, 2 * CACHE), F32),
            pltpu.SemaphoreType.DMA((DEC_DEV,)),
        ],
        compiler_params=pltpu.CompilerParams(vmem_limit_bytes=48 * 2**20),
    )(
        table.reshape(-1),
        length,
        *rates,
        *chunks,
        weight,
        keys,
        values,
        state,
        decode_memory.reshape(DEC_DEV, HD, HD),
        pages.reshape(DEC_DEV * PAGES, 2 * PAGE, HD),
    )


def second_part(rates, chunks, weight, keys, values, memory, momentum, first, tail):
    return pl.pallas_call(
        second_kernel,
        out_shape=(
            jax.ShapeDtypeStruct((ROWS, HD), BF16),
            jax.ShapeDtypeStruct((HD, HD), F32),
            jax.ShapeDtypeStruct((HD, HD), F32),
        ),
        in_specs=[IN_SMEM] * 3 + [IN_VMEM] * 11,
        out_specs=(IN_VMEM,) * 3,
        scratch_shapes=[pltpu.VMEM((HALF, 3 * HD), BF16)],
        compiler_params=pltpu.CompilerParams(vmem_limit_bytes=16 * 2**20),
    )(*rates, *chunks, weight, keys, values, memory, momentum, first, tail)


def pair_up(piece):
    z_hi = lax.axis_index("row") % 2
    other = permute(piece, lambda x, y, z_hi, z_lo, core: (x, y, 1 - z_hi, z_lo, core))
    return jnp.concatenate(
        [jnp.where(z_hi == 0, piece, other), jnp.where(z_hi == 0, other, piece)], axis=1
    )


def spread_rows(pair):
    came = [
        permute(
            pair,
            lambda x, y, z_hi, z_lo, core, step=step: (x, (y + step) % 4, z_hi, z_lo, core),
        )
        for step in (1, 2, 3)
    ]
    return [pair, *came]


def gather_weight(block):
    y = lax.axis_index("row") // 2
    x = lax.axis_index("col") // 4
    z_lo = lax.axis_index("col") // 2 % 2
    core = lax.axis_index("col") % 2
    other = permute(block, lambda x, y, z_hi, z_lo, core: (x, y, z_hi, 1 - z_lo, core))
    pair = jnp.stack(
        [jnp.where(z_lo == 0, block, other), jnp.where(z_lo == 0, other, block)], axis=0
    )
    shifted = [pair]
    for step in (1, 2, 3):
        shifted.append(
            permute(
                pair,
                lambda x, y, z_hi, z_lo, core, step=step: ((x + step) % 4, y, z_hi, z_lo, core),
            )
        )
    ordered = []
    for place in range(4):
        chosen = shifted[3]
        for step in (0, 1, 2):
            chosen = jnp.where((2 * x - y + place) % 4 == step, shifted[step], chosen)
        ordered.append(chosen)
    mine = jnp.stack(ordered, axis=0)
    theirs = permute(mine, lambda x, y, z_hi, z_lo, core: (x, y, z_hi, z_lo, 1 - core))
    both = jnp.stack(
        [jnp.where(core == 0, mine, theirs), jnp.where(core == 0, theirs, mine)], axis=2
    )
    return both.reshape(-1, block.shape[1])


def deal_states(memory_in, momentum_in, destination):
    slots = 16
    mark = jnp.broadcast_to(destination.astype(F32).reshape(1, 1, 1), (slots, 8, HD))
    pieces = jnp.concatenate(
        [memory_in.reshape(slots, 8, HD), momentum_in.reshape(slots, 8, HD), mark], axis=1
    )
    spread = lax.all_to_all(pieces, "col", split_axis=0, concat_axis=0, tiled=True)
    target = spread[:, 16, 0].astype(jnp.int32)
    chosen = target[None, :] == jnp.arange(slots, dtype=jnp.int32)[:, None]
    return jnp.sum(jnp.where(chosen[:, :, None, None], spread[None, :, :16, :], 0.0), axis=1)


def shards(
    tokens,
    qkv_weight,
    persistent,
    cache_pages,
    page_table,
    cache_len,
    destination,
    memory_in,
    momentum_in,
    forget_rate,
    keep_rate,
    learn_rate,
    decode_memory,
):
    core = lax.axis_index("col") % 2
    lower, upper = tokens[:ROWS], tokens[ROWS:]
    kept = jnp.where(core == 0, lower, upper)
    sent = jnp.where(core == 0, upper, lower)
    came = permute(sent, lambda x, y, z_hi, z_lo, core: (x, y, z_hi, z_lo, 1 - core))
    came, memory_in, momentum_in, qkv_weight = lax.optimization_barrier(
        (came, memory_in, momentum_in, qkv_weight)
    )
    own = jnp.concatenate(
        [jnp.where(core == 0, kept, came), jnp.where(core == 0, came, kept)], axis=1
    )
    parts = [
        jnp.concatenate([own[:HALF], jnp.pad(own[PCH:], ((0, PADDED - ROWS), (0, 0)))], axis=0),
        own[HALF:PCH],
    ]
    turned = [
        permute(part, lambda x, y, z_hi, z_lo, core: (y, (x + y) % 4, z_lo, z_hi, core))
        for part in parts
    ]
    pairs = [pair_up(part) for part in turned]
    weight = gather_weight(qkv_weight)
    chunks = [spread_rows(pair) for pair in pairs]
    dealt = deal_states(memory_in, momentum_in, destination)
    dealt, chunks[0][1] = lax.optimization_barrier((dealt, chunks[0][1]))
    state = lax.all_to_all(dealt, "col", split_axis=0, concat_axis=0, tiled=True)
    rates = [rate.reshape(-1) for rate in (forget_rate, keep_rate, learn_rate)]
    keys, values = persistent[:, 0], persistent[:, 1]
    first, tail, memory, momentum = first_part(
        page_table,
        cache_len,
        rates,
        chunks[0],
        weight,
        keys,
        values,
        state,
        decode_memory,
        cache_pages,
    )
    heads_out, memory, momentum = second_part(
        rates, chunks[1], weight, keys, values, memory, momentum, first, tail
    )
    return heads_out, memory[None, None], momentum[None, None]


def solution(mesh):
    placed = (
        P("row", "col"),
        P("col", "row"),
        P(None, None, "row"),
        P("col", None, None, "row"),
        P("col", None),
        P("col"),
        P("col"),
        P("col", "row", None, None),
        P("col", "row", None, None),
        P("col", "row", None),
        P("col", "row", None),
        P("col", "row", None),
        P("col", "row", None, None),
    )
    return jax.shard_map(
        shards,
        mesh=mesh,
        in_specs=placed,
        out_specs=(P("col", "row"), P("col", "row", None, None), P("col", "row", None, None)),
        check_vma=False,
    )
```

```python
import jax
import jax.numpy as jnp
from jax import lax
from jax.experimental import pallas as pl
from jax.experimental.pallas import tpu as pltpu
from jax.sharding import PartitionSpec as P

HD = 128
PERS = 16
MCH = 64
PCH = 1024
DEC_DEV = 4
CACHE = 4096
PAGE = 256
PAGES = CACHE // PAGE
ROWS = PCH + DEC_DEV
PADDED = PCH + 16

F32 = jnp.float32
BF16 = jnp.bfloat16
EPSILON = 1e-6
SCALE = HD**-0.5


def device_at(x, y, z_hi, z_lo, core):
    return (2 * y + z_hi) * 16 + 4 * x + 2 * z_lo + core


def moves(target):
    pairs = []
    for x in range(4):
        for y in range(4):
            for z_hi in range(2):
                for z_lo in range(2):
                    for core in range(2):
                        here = (x, y, z_hi, z_lo, core)
                        pairs.append((device_at(*here), device_at(*target(*here))))
    return pairs


def permute(values, target):
    return lax.ppermute(values, ("row", "col"), moves(target))


def dot_f32(left, right):
    return lax.dot_general(left, right, (((1,), (0,)), ((), ())), preferred_element_type=F32)


def dot_rows(left, right):
    return lax.dot_general(left, right, (((1,), (1,)), ((), ())), preferred_element_type=F32)


def dot_turned(left, right):
    return lax.dot_general(left, right, (((0,), (0,)), ((), ())), preferred_element_type=F32)


def two_parts(values):
    high = values.astype(BF16)
    return jnp.concatenate([high, (values - high.astype(F32)).astype(BF16)], axis=0)


def inverse_norm(rows):
    wide = rows.astype(F32)
    return lax.rsqrt(jnp.sum(wide * wide, axis=-1, keepdims=True) + EPSILON)


HALF = PCH // 2
EXTRA = PADDED - PCH
STATE = 3 * MCH
MARK = STATE + 2 * HD
PACKET = MARK + 16


def step_weight(step, near_ref, far_ref):
    tiles = []
    for tile in range(3):
        rows = slice(tile * MCH, tile * MCH + MCH)
        parts = [ref[step, place, rows, :] for place in range(2) for ref in (near_ref, far_ref)]
        tiles.append(jnp.concatenate(parts, axis=0))
    return jnp.concatenate(tiles, axis=1)


def project(token_refs, near_ref, far_ref):
    total = None
    x, y = lax.axis_index("col") // 4, lax.axis_index("row") // 2
    for step, token_ref in enumerate(token_refs):
        moved = lax.rem(2 * x + step + 4 - y, 4)
        part = dot_f32(token_ref[...], step_weight(moved, near_ref, far_ref))
        total = part if total is None else total + part
    return total.astype(BF16)


def own_states(column, packet_refs):
    total = jnp.zeros((2 * HD, HD), F32)
    for packet_ref in packet_refs:
        for step in range(4):
            for place in range(2):
                mark = packet_ref[step, place, MARK : MARK + 16, :].astype(F32)[0:1]
                state = packet_ref[step, place, STATE : STATE + 2 * HD, :].astype(F32)
                total = total + jnp.where(mark == column, state, 0.0)
    return total[:HD], total[HD:]


def prefill(
    first, projected, persist_key, persist_value, memory, momentum, rates, out_ref, out_at
):
    forget_ref, keep_ref, learn_ref = rates
    blank = jnp.zeros((HD - MCH - PERS, HD), BF16)
    row_at = lax.broadcasted_iota(jnp.int32, (MCH, HD), 0)
    column_at = lax.broadcasted_iota(jnp.int32, (MCH, HD), 1)
    visible = (column_at <= row_at) | ((column_at >= MCH) & (column_at < MCH + PERS))
    for step in range(HALF // MCH):
        block = first + step
        here = slice(step * MCH, step * MCH + MCH)
        query = projected[here, 0:HD]
        key = projected[here, HD : 2 * HD]
        value = projected[here, 2 * HD : 3 * HD]
        query_scale = inverse_norm(query)
        key_scale = inverse_norm(key)
        left = jnp.concatenate(
            [jnp.concatenate([query, query], axis=1), jnp.concatenate([key, key], axis=1)], axis=0
        )
        reads = dot_f32(left, two_parts(memory))
        errors = reads[MCH:] * key_scale - value.astype(F32)
        errors = errors * (key_scale * (2.0 / MCH))
        gradient = dot_turned(jnp.concatenate([key, key], axis=0), two_parts(errors))
        momentum = keep_ref[block] * momentum - learn_ref[block] * gradient
        memory = (1.0 - forget_ref[block]) * memory + momentum

        keys = jnp.concatenate([key, persist_key, blank], axis=0)
        values = jnp.concatenate([value, persist_value, blank], axis=0)
        scores = jnp.where(visible, dot_rows(query, keys) * SCALE, -jnp.inf)
        powers = jnp.exp(scores - jnp.max(scores, axis=-1, keepdims=True))
        weights = (powers / jnp.sum(powers, axis=-1, keepdims=True)).astype(BF16)
        result = dot_f32(weights, values) + reads[:MCH] * query_scale
        out_ref[out_at + step * MCH : out_at + step * MCH + MCH, :] = result.astype(BF16)
    return memory, momentum


def decode(
    whole_ref, projected, persist_key, persist_value, decode_memory_ref, cache, score, arrival
):
    query = projected[HALF : HALF + EXTRA, 0:HD]
    key = projected[HALF : HALF + EXTRA, HD : 2 * HD]
    value = projected[HALF : HALF + EXTRA, 2 * HD : 3 * HD]
    row = lax.broadcasted_iota(jnp.int32, (EXTRA, 1), 0)
    length = jnp.zeros((EXTRA, 1), jnp.int32)
    for request in range(DEC_DEV):
        pltpu.make_async_copy(cache.at[request], cache.at[request], arrival.at[request]).wait()
        length = jnp.where(row == request, whole_ref[DEC_DEV * PAGES + request], length)
    for place in range(PAGES):
        span = slice(place * 2 * PAGE, place * 2 * PAGE + 2 * PAGE)
        found = dot_rows(query, cache[0, span, :])
        for request in range(1, DEC_DEV):
            found = jnp.where(row == request, dot_rows(query, cache[request, span, :]), found)
        column = lax.broadcasted_iota(jnp.int32, (EXTRA, 2 * PAGE), 1)
        live = ((column & 1) == 0) & ((column >> 1) + place * PAGE < length)
        score[:, span] = jnp.where(live, found * SCALE, -jnp.inf)
    own_score = jnp.sum(query.astype(F32) * key.astype(F32), axis=-1, keepdims=True) * SCALE
    persist_score = dot_rows(query, persist_key) * SCALE
    cache_score = score[...]
    largest = jnp.maximum(
        jnp.maximum(jnp.max(cache_score, axis=-1, keepdims=True), own_score),
        jnp.max(persist_score, axis=-1, keepdims=True),
    )
    cache_power = jnp.exp(cache_score - largest)
    own_power = jnp.exp(own_score - largest)
    persist_power = jnp.exp(persist_score - largest)
    totals = (
        jnp.sum(cache_power, axis=-1, keepdims=True)
        + own_power
        + jnp.sum(persist_power, axis=-1, keepdims=True)
    )
    share = 1.0 / totals
    cache_weight = pltpu.roll(cache_power * share, 1, 1).astype(BF16)
    attended = jnp.zeros((EXTRA, HD), F32)
    for request in range(DEC_DEV):
        attended = jnp.where(row == request, dot_f32(cache_weight, cache[request]), attended)
    own_weight = (own_power * share).astype(BF16).astype(F32)
    attended = attended + own_weight * value.astype(F32)
    attended = attended + dot_f32((persist_power * share).astype(BF16), persist_value)
    twice = jnp.concatenate([query, query], axis=1)
    readout = jnp.zeros((EXTRA, HD), F32)
    for request in range(DEC_DEV):
        read = dot_f32(twice, decode_memory_ref[request])
        readout = jnp.where(row == request, read, readout)
    return (attended + readout * inverse_norm(query)).astype(BF16)


class Rate:
    def __init__(self, rates_ref, kind):
        self.rates_ref, self.start = rates_ref, kind * (PCH // MCH)

    def __getitem__(self, block):
        return self.rates_ref[self.start + block]


def first_kernel(*refs):
    token_refs, packet_refs = refs[0:4], refs[4:6]
    whole_ref, rates_ref, persist_ref, decode_memory_ref, page_ref = refs[6:11]
    out_ref, tail_ref, memory_ref, momentum_ref = refs[11:15]
    projected, cache, score, arrival = refs[15:]
    for request in range(DEC_DEV):
        for place in range(PAGES):
            pltpu.make_async_copy(
                page_ref.at[whole_ref[request * PAGES + place]],
                cache.at[request, pl.ds(place * 2 * PAGE, 2 * PAGE)],
                arrival.at[request],
            ).start()
    projected[...] = project(token_refs, *packet_refs)
    memory, momentum = own_states(lax.axis_index("col").astype(F32), packet_refs)
    persist_key, persist_value = persist_ref[0:PERS, :], persist_ref[PERS:, :]
    rates = [Rate(rates_ref, kind) for kind in range(3)]
    memory, momentum = prefill(
        0, projected, persist_key, persist_value, memory, momentum, rates, out_ref, 0
    )
    memory_ref[...] = memory
    momentum_ref[...] = momentum
    tail_ref[...] = decode(
        whole_ref, projected, persist_key, persist_value, decode_memory_ref, cache, score, arrival
    )


def second_kernel(*refs):
    token_refs, packet_refs, rates_ref, persist_ref = refs[0:4], refs[4:6], refs[6], refs[7]
    memory_in_ref, momentum_in_ref, first_ref, tail_ref = refs[8:12]
    out_ref, memory_ref, momentum_ref, projected = refs[12:]
    projected[...] = project(token_refs, *packet_refs)
    memory, momentum = prefill(
        HALF // MCH,
        projected,
        persist_ref[0:PERS, :],
        persist_ref[PERS:, :],
        memory_in_ref[...],
        momentum_in_ref[...],
        [Rate(rates_ref, kind) for kind in range(3)],
        out_ref,
        HALF,
    )
    memory_ref[...] = memory
    momentum_ref[...] = momentum
    out_ref[0:HALF, :] = first_ref[...]
    out_ref[PCH:ROWS, :] = tail_ref[0:DEC_DEV, :]


IN_SMEM = pl.BlockSpec(memory_space=pltpu.SMEM)
IN_VMEM = pl.BlockSpec(memory_space=pltpu.VMEM)


IN_HBM = pl.BlockSpec(memory_space=pltpu.HBM)


def first_part(whole, rates, chunks, packets, persist, decode_memory, pages):
    return pl.pallas_call(
        first_kernel,
        out_shape=(
            jax.ShapeDtypeStruct((HALF, HD), BF16),
            jax.ShapeDtypeStruct((EXTRA, HD), BF16),
            jax.ShapeDtypeStruct((HD, HD), F32),
            jax.ShapeDtypeStruct((HD, HD), F32),
        ),
        in_specs=[IN_VMEM] * 6 + [IN_SMEM] * 2 + [IN_VMEM] * 2 + [IN_HBM],
        out_specs=(IN_VMEM,) * 4,
        scratch_shapes=[
            pltpu.VMEM((HALF + EXTRA, 3 * HD), BF16),
            pltpu.VMEM((DEC_DEV, 2 * CACHE, HD), BF16),
            pltpu.VMEM((EXTRA, 2 * CACHE), F32),
            pltpu.SemaphoreType.DMA((DEC_DEV,)),
        ],
        compiler_params=pltpu.CompilerParams(vmem_limit_bytes=46 * 2**20),
    )(
        *chunks,
        *packets,
        whole,
        rates,
        persist,
        decode_memory,
        pages.reshape(DEC_DEV * PAGES, 2 * PAGE, HD),
    )


def second_part(rates, chunks, packets, persist, memory, momentum, first, tail):
    return pl.pallas_call(
        second_kernel,
        out_shape=(
            jax.ShapeDtypeStruct((ROWS, HD), BF16),
            jax.ShapeDtypeStruct((HD, HD), F32),
            jax.ShapeDtypeStruct((HD, HD), F32),
        ),
        in_specs=[IN_VMEM] * 6 + [IN_SMEM] + [IN_VMEM] * 5,
        out_specs=(IN_VMEM,) * 3,
        scratch_shapes=[pltpu.VMEM((HALF, 3 * HD), BF16)],
        compiler_params=pltpu.CompilerParams(vmem_limit_bytes=16 * 2**20),
    )(*chunks, *packets, rates, persist, memory, momentum, first, tail)


def pair_up(piece):
    other = permute(piece, lambda x, y, z_hi, z_lo, core: (x, y, 1 - z_hi, z_lo, core))
    return jnp.concatenate([piece, other], axis=1)


def spread_rows(pair):
    came = [
        permute(
            pair,
            lambda x, y, z_hi, z_lo, core, step=step: (x, (y + step) % 4, z_hi, z_lo, core),
        )
        for step in (1, 2, 3)
    ]
    return [pair, *came]


def packet_kernel(destination_ref, weight_ref, memory_ref, momentum_ref, packet_ref):
    for tile in range(3):
        packet_ref[tile * MCH : tile * MCH + MCH, :] = weight_ref[:, tile * HD : tile * HD + HD]
    states = jnp.concatenate([memory_ref[...], momentum_ref[...]], axis=0)
    high = states.astype(BF16)
    packet_ref[STATE : STATE + 2 * HD, :] = high
    packet_ref[MARK:PACKET, :] = jnp.full((16, HD), destination_ref[0].astype(F32)).astype(BF16)


def make_packet(weight, memory_in, momentum_in, destination):
    return pl.pallas_call(
        packet_kernel,
        out_shape=jax.ShapeDtypeStruct((PACKET, HD), BF16),
        in_specs=[IN_SMEM] + [IN_VMEM] * 3,
        out_specs=IN_VMEM,
    )(destination, weight, memory_in.reshape(HD, HD), momentum_in.reshape(HD, HD))


def gather_packets(packet, turned):
    same = lax.axis_index("row") % 2 == lax.axis_index("col") // 2 % 2
    other = permute(packet, lambda x, y, z_hi, z_lo, core: (x, y, z_hi, 1 - z_lo, core))
    pair = jnp.stack([jnp.where(same, packet, other), jnp.where(same, other, packet)], axis=0)
    pair, turned = lax.optimization_barrier((pair, turned))
    near = [pair]
    for step in (1, 2, 3):
        near.append(
            permute(
                pair,
                lambda x, y, z_hi, z_lo, core, step=step: ((x + step) % 4, y, z_hi, z_lo, core),
            )
        )
    near = jnp.stack(near, axis=0)
    far = permute(near, lambda x, y, z_hi, z_lo, core: (x, y, z_hi, z_lo, 1 - core))
    return (near, far), turned


def shards(
    tokens,
    qkv_weight,
    persistent,
    cache_pages,
    page_table,
    cache_len,
    destination,
    memory_in,
    momentum_in,
    forget_rate,
    keep_rate,
    learn_rate,
    decode_memory,
):
    core = lax.axis_index("col") % 2
    lower, upper = tokens[:ROWS], tokens[ROWS:]
    kept = jnp.where(core == 0, lower, upper)
    sent = jnp.where(core == 0, upper, lower)
    came = permute(sent, lambda x, y, z_hi, z_lo, core: (x, y, z_hi, z_lo, 1 - core))
    own = jnp.concatenate([kept, came], axis=1)
    (
        own,
        persistent,
        page_table,
        cache_len,
        forget_rate,
        keep_rate,
        learn_rate,
        decode_memory,
    ) = lax.optimization_barrier(
        (
            own,
            persistent,
            page_table,
            cache_len,
            forget_rate,
            keep_rate,
            learn_rate,
            decode_memory,
        )
    )
    parts = [
        jnp.concatenate([own[:HALF], jnp.pad(own[PCH:], ((0, PADDED - ROWS), (0, 0)))], axis=0),
        own[HALF:PCH],
    ]
    turned = permute(
        jnp.concatenate(parts, axis=0),
        lambda x, y, z_hi, z_lo, core: (y, (x + y) % 4, z_lo, z_hi, core),
    )
    packets, turned = gather_packets(
        make_packet(qkv_weight, memory_in, momentum_in, destination), turned
    )
    pair = pair_up(turned)
    pairs = [pair[: HALF + EXTRA], pair[HALF + EXTRA :]]
    chunks = [spread_rows(pair) for pair in pairs]
    rates = jnp.concatenate(
        [rate.reshape(-1) for rate in (forget_rate, keep_rate, learn_rate)], axis=0
    )
    whole = jnp.concatenate([page_table.reshape(-1), cache_len], axis=0)
    persist = jnp.concatenate([persistent[:, 0], persistent[:, 1]], axis=0)
    decode_memory = decode_memory.reshape(DEC_DEV, HD, HD)
    high = decode_memory.astype(BF16)
    decode_parts = jnp.concatenate(
        [high, (decode_memory - high.astype(F32)).astype(BF16)], axis=1
    )
    first, tail, memory, momentum = first_part(
        whole,
        rates,
        chunks[0],
        packets,
        persist,
        decode_parts,
        cache_pages,
    )
    heads_out, memory, momentum = second_part(
        rates, chunks[1], packets, persist, memory, momentum, first, tail
    )
    return heads_out, memory[None, None], momentum[None, None]


def solution(mesh):
    placed = (
        P("row", "col"),
        P("col", "row"),
        P(None, None, "row"),
        P("col", None, None, "row"),
        P("col", None),
        P("col"),
        P("col"),
        P("col", "row", None, None),
        P("col", "row", None, None),
        P("col", "row", None),
        P("col", "row", None),
        P("col", "row", None),
        P("col", "row", None, None),
    )
    return jax.shard_map(
        shards,
        mesh=mesh,
        in_specs=placed,
        out_specs=(P("col", "row"), P("col", "row", None, None), P("col", "row", None, None)),
        check_vma=False,
    )
```

```python
import jax
import jax.numpy as jnp
from jax import lax
from jax.experimental import pallas as pl
from jax.experimental.pallas import tpu as pltpu
from jax.sharding import PartitionSpec as P

HD = 128
PERS = 16
MCH = 64
PCH = 1024
DEC_DEV = 4
CACHE = 4096
PAGE = 256
PAGES = CACHE // PAGE
ROWS = PCH + DEC_DEV
PADDED = PCH + 16

F32 = jnp.float32
BF16 = jnp.bfloat16
EPSILON = 1e-6
SCALE = HD**-0.5


def device_at(x, y, z_hi, z_lo, core):
    return (2 * y + z_hi) * 16 + 4 * x + 2 * z_lo + core


def moves(target):
    pairs = []
    for x in range(4):
        for y in range(4):
            for z_hi in range(2):
                for z_lo in range(2):
                    for core in range(2):
                        here = (x, y, z_hi, z_lo, core)
                        pairs.append((device_at(*here), device_at(*target(*here))))
    return pairs


def permute(values, target):
    return lax.ppermute(values, ("row", "col"), moves(target))


def dot_f32(left, right):
    return lax.dot_general(left, right, (((1,), (0,)), ((), ())), preferred_element_type=F32)


def dot_rows(left, right):
    return lax.dot_general(left, right, (((1,), (1,)), ((), ())), preferred_element_type=F32)


def dot_turned(left, right):
    return lax.dot_general(left, right, (((0,), (0,)), ((), ())), preferred_element_type=F32)


def two_parts(values):
    high = values.astype(BF16)
    return jnp.concatenate([high, (values - high.astype(F32)).astype(BF16)], axis=0)


def inverse_norm(rows):
    wide = rows.astype(F32)
    return lax.rsqrt(jnp.sum(wide * wide, axis=-1, keepdims=True) + EPSILON)


HALF = 576
REST = PCH - HALF
EXTRA = PADDED - PCH
STATE = 3 * MCH
MARK = STATE + 2 * HD
PACKET = MARK + 16


def step_weight(step, near_ref, far_ref):
    tiles = []
    for tile in range(3):
        rows = slice(tile * MCH, tile * MCH + MCH)
        parts = [ref[step, place, rows, :] for place in range(2) for ref in (near_ref, far_ref)]
        tiles.append(jnp.concatenate(parts, axis=0))
    return jnp.concatenate(tiles, axis=1)


def project(token_refs, near_ref, far_ref):
    total = None
    x, y = lax.axis_index("col") // 4, lax.axis_index("row") // 2
    for step, token_ref in enumerate(token_refs):
        moved = lax.rem(2 * x + step + 4 - y, 4)
        part = dot_f32(token_ref[...], step_weight(moved, near_ref, far_ref))
        total = part if total is None else total + part
    return total.astype(BF16)


def own_states(column, packet_refs):
    total = jnp.zeros((2 * HD, HD), F32)
    for packet_ref in packet_refs:
        for step in range(4):
            for place in range(2):
                mark = packet_ref[step, place, MARK : MARK + 16, :].astype(F32)[0:1]
                state = packet_ref[step, place, STATE : STATE + 2 * HD, :].astype(F32)
                total = total + jnp.where(mark == column, state, 0.0)
    return total[:HD], total[HD:]


def prefill(
    first, count, projected, persist_key, persist_value, memory, momentum, rates, out_ref, out_at
):
    forget_ref, keep_ref, learn_ref = rates
    blank = jnp.zeros((HD - MCH - PERS, HD), BF16)
    row_at = lax.broadcasted_iota(jnp.int32, (MCH, HD), 0)
    column_at = lax.broadcasted_iota(jnp.int32, (MCH, HD), 1)
    visible = (column_at <= row_at) | ((column_at >= MCH) & (column_at < MCH + PERS))
    for step in range(count):
        block = first + step
        here = slice(step * MCH, step * MCH + MCH)
        query = projected[here, 0:HD]
        key = projected[here, HD : 2 * HD]
        value = projected[here, 2 * HD : 3 * HD]
        query_scale = inverse_norm(query)
        key_scale = inverse_norm(key)
        left = jnp.concatenate(
            [jnp.concatenate([query, query], axis=1), jnp.concatenate([key, key], axis=1)], axis=0
        )
        reads = dot_f32(left, two_parts(memory))
        errors = reads[MCH:] * key_scale - value.astype(F32)
        errors = errors * (key_scale * (2.0 / MCH))
        gradient = dot_turned(jnp.concatenate([key, key], axis=0), two_parts(errors))
        momentum = keep_ref[block] * momentum - learn_ref[block] * gradient
        memory = (1.0 - forget_ref[block]) * memory + momentum

        keys = jnp.concatenate([key, persist_key, blank], axis=0)
        values = jnp.concatenate([value, persist_value, blank], axis=0)
        scores = jnp.where(visible, dot_rows(query, keys) * SCALE, -jnp.inf)
        powers = jnp.exp(scores - jnp.max(scores, axis=-1, keepdims=True))
        weights = (powers / jnp.sum(powers, axis=-1, keepdims=True)).astype(BF16)
        result = dot_f32(weights, values) + reads[:MCH] * query_scale
        out_ref[out_at + step * MCH : out_at + step * MCH + MCH, :] = result.astype(BF16)
    return memory, momentum


def decode(
    whole_ref, projected, persist_key, persist_value, decode_memory_ref, cache, score
):
    query = projected[HALF : HALF + EXTRA, 0:HD]
    key = projected[HALF : HALF + EXTRA, HD : 2 * HD]
    value = projected[HALF : HALF + EXTRA, 2 * HD : 3 * HD]
    row = lax.broadcasted_iota(jnp.int32, (EXTRA, 1), 0)
    length = jnp.zeros((EXTRA, 1), jnp.int32)
    for request in range(DEC_DEV):
        length = jnp.where(row == request, whole_ref[DEC_DEV * PAGES + request], length)
    for place in range(PAGES):
        span = slice(place * 2 * PAGE, place * 2 * PAGE + 2 * PAGE)
        found = dot_rows(query, cache[0, span, :])
        for request in range(1, DEC_DEV):
            found = jnp.where(row == request, dot_rows(query, cache[request, span, :]), found)
        column = lax.broadcasted_iota(jnp.int32, (EXTRA, 2 * PAGE), 1)
        live = ((column & 1) == 0) & ((column >> 1) + place * PAGE < length)
        score[:, span] = jnp.where(live, found * SCALE, -jnp.inf)
    own_score = jnp.sum(query.astype(F32) * key.astype(F32), axis=-1, keepdims=True) * SCALE
    persist_score = dot_rows(query, persist_key) * SCALE
    cache_score = score[...]
    largest = jnp.maximum(
        jnp.maximum(jnp.max(cache_score, axis=-1, keepdims=True), own_score),
        jnp.max(persist_score, axis=-1, keepdims=True),
    )
    cache_power = jnp.exp(cache_score - largest)
    own_power = jnp.exp(own_score - largest)
    persist_power = jnp.exp(persist_score - largest)
    totals = (
        jnp.sum(cache_power, axis=-1, keepdims=True)
        + own_power
        + jnp.sum(persist_power, axis=-1, keepdims=True)
    )
    share = 1.0 / totals
    cache_weight = pltpu.roll(cache_power * share, 1, 1).astype(BF16)
    attended = jnp.zeros((EXTRA, HD), F32)
    for request in range(DEC_DEV):
        attended = jnp.where(row == request, dot_f32(cache_weight, cache[request]), attended)
    own_weight = (own_power * share).astype(BF16).astype(F32)
    attended = attended + own_weight * value.astype(F32)
    attended = attended + dot_f32((persist_power * share).astype(BF16), persist_value)
    twice = jnp.concatenate([query, query], axis=1)
    readout = jnp.zeros((EXTRA, HD), F32)
    for request in range(DEC_DEV):
        read = dot_f32(twice, decode_memory_ref[request])
        readout = jnp.where(row == request, read, readout)
    return (attended + readout * inverse_norm(query)).astype(BF16)


class Rate:
    def __init__(self, rates_ref, kind):
        self.rates_ref, self.start = rates_ref, kind * (PCH // MCH)

    def __getitem__(self, block):
        return self.rates_ref[self.start + block]


def first_kernel(*refs):
    token_refs, packet_refs = refs[0:4], refs[4:6]
    whole_ref, rates_ref, persist_ref, decode_memory_ref, cache = refs[6:11]
    out_ref, tail_ref, memory_ref, momentum_ref = refs[11:15]
    projected, score = refs[15:]
    projected[...] = project(token_refs, *packet_refs)
    memory, momentum = own_states(lax.axis_index("col").astype(F32), packet_refs)
    persist_key, persist_value = persist_ref[0:PERS, :], persist_ref[PERS:, :]
    rates = [Rate(rates_ref, kind) for kind in range(3)]
    memory, momentum = prefill(
        0, HALF // MCH, projected, persist_key, persist_value, memory, momentum, rates, out_ref, 0
    )
    memory_ref[...] = memory
    momentum_ref[...] = momentum
    tail_ref[...] = decode(
        whole_ref, projected, persist_key, persist_value, decode_memory_ref, cache, score
    )


def second_kernel(*refs):
    token_refs, packet_refs, rates_ref, persist_ref = refs[0:4], refs[4:6], refs[6], refs[7]
    memory_in_ref, momentum_in_ref, first_ref, tail_ref = refs[8:12]
    out_ref, memory_ref, momentum_ref, projected = refs[12:]
    projected[...] = project(token_refs, *packet_refs)
    memory, momentum = prefill(
        HALF // MCH,
        REST // MCH,
        projected,
        persist_ref[0:PERS, :],
        persist_ref[PERS:, :],
        memory_in_ref[...],
        momentum_in_ref[...],
        [Rate(rates_ref, kind) for kind in range(3)],
        out_ref,
        HALF,
    )
    memory_ref[...] = memory
    momentum_ref[...] = momentum
    out_ref[0:HALF, :] = first_ref[...]
    out_ref[PCH:ROWS, :] = tail_ref[0:DEC_DEV, :]


IN_SMEM = pl.BlockSpec(memory_space=pltpu.SMEM)
IN_VMEM = pl.BlockSpec(memory_space=pltpu.VMEM)


IN_HBM = pl.BlockSpec(memory_space=pltpu.HBM)


def page_kernel(whole_ref, page_ref, cache_ref, arrival):
    for request in range(DEC_DEV):
        for place in range(PAGES):
            pltpu.make_async_copy(
                page_ref.at[whole_ref[request * PAGES + place]],
                cache_ref.at[request, pl.ds(place * 2 * PAGE, 2 * PAGE)],
                arrival.at[request],
            ).start()
    for request in range(DEC_DEV):
        whole = cache_ref.at[request]
        pltpu.make_async_copy(whole, whole, arrival.at[request]).wait()


def order_pages(whole, pages):
    return pl.pallas_call(
        page_kernel,
        out_shape=jax.ShapeDtypeStruct((DEC_DEV, 2 * CACHE, HD), BF16),
        in_specs=[IN_SMEM, IN_HBM],
        out_specs=IN_VMEM,
        scratch_shapes=[pltpu.SemaphoreType.DMA((DEC_DEV,))],
        compiler_params=pltpu.CompilerParams(vmem_limit_bytes=42 * 2**20),
    )(whole, pages.reshape(DEC_DEV * PAGES, 2 * PAGE, HD))


def first_part(whole, rates, chunks, packets, persist, decode_memory, cache):
    return pl.pallas_call(
        first_kernel,
        out_shape=(
            jax.ShapeDtypeStruct((HALF, HD), BF16),
            jax.ShapeDtypeStruct((EXTRA, HD), BF16),
            jax.ShapeDtypeStruct((HD, HD), F32),
            jax.ShapeDtypeStruct((HD, HD), F32),
        ),
        in_specs=[IN_VMEM] * 6 + [IN_SMEM] * 2 + [IN_VMEM] * 3,
        out_specs=(IN_VMEM,) * 4,
        scratch_shapes=[
            pltpu.VMEM((HALF + EXTRA, 3 * HD), BF16),
            pltpu.VMEM((EXTRA, 2 * CACHE), F32),
        ],
        compiler_params=pltpu.CompilerParams(vmem_limit_bytes=16 * 2**20),
    )(
        *chunks,
        *packets,
        whole,
        rates,
        persist,
        decode_memory,
        cache,
    )


def second_part(rates, chunks, packets, persist, memory, momentum, first, tail):
    return pl.pallas_call(
        second_kernel,
        out_shape=(
            jax.ShapeDtypeStruct((ROWS, HD), BF16),
            jax.ShapeDtypeStruct((HD, HD), F32),
            jax.ShapeDtypeStruct((HD, HD), F32),
        ),
        in_specs=[IN_VMEM] * 6 + [IN_SMEM] + [IN_VMEM] * 5,
        out_specs=(IN_VMEM,) * 3,
        scratch_shapes=[pltpu.VMEM((REST, 3 * HD), BF16)],
        compiler_params=pltpu.CompilerParams(vmem_limit_bytes=16 * 2**20),
    )(*chunks, *packets, rates, persist, memory, momentum, first, tail)


def pair_up(piece):
    other = permute(piece, lambda x, y, z_hi, z_lo, core: (x, y, 1 - z_hi, z_lo, core))
    return jnp.concatenate([piece, other], axis=1)


def spread_rows(pair):
    came = [
        permute(
            pair,
            lambda x, y, z_hi, z_lo, core, step=step: (x, (y + step) % 4, z_hi, z_lo, core),
        )
        for step in (1, 2, 3)
    ]
    return [pair, *came]


def packet_kernel(destination_ref, weight_ref, memory_ref, momentum_ref, packet_ref):
    for tile in range(3):
        packet_ref[tile * MCH : tile * MCH + MCH, :] = weight_ref[:, tile * HD : tile * HD + HD]
    states = jnp.concatenate([memory_ref[...], momentum_ref[...]], axis=0)
    high = states.astype(BF16)
    packet_ref[STATE : STATE + 2 * HD, :] = high
    packet_ref[MARK:PACKET, :] = jnp.full((16, HD), destination_ref[0].astype(F32)).astype(BF16)


def make_packet(weight, memory_in, momentum_in, destination):
    return pl.pallas_call(
        packet_kernel,
        out_shape=jax.ShapeDtypeStruct((PACKET, HD), BF16),
        in_specs=[IN_SMEM] + [IN_VMEM] * 3,
        out_specs=IN_VMEM,
    )(destination, weight, memory_in.reshape(HD, HD), momentum_in.reshape(HD, HD))


def gather_packets(packet, turned, cache):
    same = lax.axis_index("row") % 2 == lax.axis_index("col") // 2 % 2
    other = permute(packet, lambda x, y, z_hi, z_lo, core: (x, y, z_hi, 1 - z_lo, core))
    other, turned, cache = lax.optimization_barrier((other, turned, cache))
    pair = jnp.stack([jnp.where(same, packet, other), jnp.where(same, other, packet)], axis=0)
    near = [pair]
    for step in (1, 2, 3):
        near.append(
            permute(
                pair,
                lambda x, y, z_hi, z_lo, core, step=step: ((x + step) % 4, y, z_hi, z_lo, core),
            )
        )
    near = jnp.stack(near, axis=0)
    far = permute(near, lambda x, y, z_hi, z_lo, core: (x, y, z_hi, z_lo, 1 - core))
    return (near, far), turned, cache


def shards(
    tokens,
    qkv_weight,
    persistent,
    cache_pages,
    page_table,
    cache_len,
    destination,
    memory_in,
    momentum_in,
    forget_rate,
    keep_rate,
    learn_rate,
    decode_memory,
):
    core = lax.axis_index("col") % 2
    lower, upper = tokens[:ROWS], tokens[ROWS:]
    kept = jnp.where(core == 0, lower, upper)
    sent = jnp.where(core == 0, upper, lower)
    came = permute(sent, lambda x, y, z_hi, z_lo, core: (x, y, z_hi, z_lo, 1 - core))
    own = jnp.concatenate([kept, came], axis=1)
    (
        own,
        persistent,
        page_table,
        cache_len,
        forget_rate,
        keep_rate,
        learn_rate,
        decode_memory,
    ) = lax.optimization_barrier(
        (
            own,
            persistent,
            page_table,
            cache_len,
            forget_rate,
            keep_rate,
            learn_rate,
            decode_memory,
        )
    )
    parts = [
        jnp.concatenate([own[:HALF], jnp.pad(own[PCH:], ((0, PADDED - ROWS), (0, 0)))], axis=0),
        own[HALF:PCH],
    ]
    turned = permute(
        jnp.concatenate(parts, axis=0),
        lambda x, y, z_hi, z_lo, core: (y, (x + y) % 4, z_lo, z_hi, core),
    )
    whole = jnp.concatenate([page_table.reshape(-1), cache_len], axis=0)
    cache = order_pages(whole, cache_pages)
    packet = make_packet(qkv_weight, memory_in, momentum_in, destination)
    packets, turned, cache = gather_packets(packet, turned, cache)
    pair = pair_up(turned)
    pairs = [pair[: HALF + EXTRA], pair[HALF + EXTRA :]]
    chunks = [spread_rows(pair) for pair in pairs]
    rates = jnp.concatenate(
        [rate.reshape(-1) for rate in (forget_rate, keep_rate, learn_rate)], axis=0
    )
    persist = jnp.concatenate([persistent[:, 0], persistent[:, 1]], axis=0)
    decode_memory = decode_memory.reshape(DEC_DEV, HD, HD)
    high = decode_memory.astype(BF16)
    decode_parts = jnp.concatenate(
        [high, (decode_memory - high.astype(F32)).astype(BF16)], axis=1
    )
    first, tail, memory, momentum = first_part(
        whole,
        rates,
        chunks[0],
        packets,
        persist,
        decode_parts,
        cache,
    )
    heads_out, memory, momentum = second_part(
        rates, chunks[1], packets, persist, memory, momentum, first, tail
    )
    return heads_out, memory[None, None], momentum[None, None]


def solution(mesh):
    placed = (
        P("row", "col"),
        P("col", "row"),
        P(None, None, "row"),
        P("col", None, None, "row"),
        P("col", None),
        P("col"),
        P("col"),
        P("col", "row", None, None),
        P("col", "row", None, None),
        P("col", "row", None),
        P("col", "row", None),
        P("col", "row", None),
        P("col", "row", None, None),
    )
    return jax.shard_map(
        shards,
        mesh=mesh,
        in_specs=placed,
        out_specs=(P("col", "row"), P("col", "row", None, None), P("col", "row", None, None)),
        check_vma=False,
    )
```

```python
import jax
import jax.numpy as jnp
from jax import lax
from jax.experimental import pallas as pl
from jax.experimental.pallas import tpu as pltpu
from jax.sharding import PartitionSpec as P

HD = 128
PERS = 16
MCH = 64
PCH = 1024
DEC_DEV = 4
CACHE = 4096
PAGE = 256
PAGES = CACHE // PAGE
ROWS = PCH + DEC_DEV
PADDED = PCH + 16

F32 = jnp.float32
BF16 = jnp.bfloat16
EPSILON = 1e-6
SCALE = HD**-0.5


def device_at(x, y, z_hi, z_lo, core):
    return (2 * y + z_hi) * 16 + 4 * x + 2 * z_lo + core


def moves(target):
    pairs = []
    for x in range(4):
        for y in range(4):
            for z_hi in range(2):
                for z_lo in range(2):
                    for core in range(2):
                        here = (x, y, z_hi, z_lo, core)
                        pairs.append((device_at(*here), device_at(*target(*here))))
    return pairs


def permute(values, target):
    return lax.ppermute(values, ("row", "col"), moves(target))


def dot_f32(left, right):
    return lax.dot_general(left, right, (((1,), (0,)), ((), ())), preferred_element_type=F32)


def dot_rows(left, right):
    return lax.dot_general(left, right, (((1,), (1,)), ((), ())), preferred_element_type=F32)


def dot_turned(left, right):
    return lax.dot_general(left, right, (((0,), (0,)), ((), ())), preferred_element_type=F32)


def two_parts(values):
    high = values.astype(BF16)
    return jnp.concatenate([high, (values - high.astype(F32)).astype(BF16)], axis=0)


def inverse_norm(rows):
    wide = rows.astype(F32)
    return lax.rsqrt(jnp.sum(wide * wide, axis=-1, keepdims=True) + EPSILON)


HALF = 640
REST = PCH - HALF
EXTRA = PADDED - PCH
STATE = 3 * MCH
MARK = STATE + 2 * HD
PACKET = MARK + 16


def step_weight(step, near_ref, far_ref):
    tiles = []
    for tile in range(3):
        rows = slice(tile * MCH, tile * MCH + MCH)
        parts = [ref[step, place, rows, :] for place in range(2) for ref in (near_ref, far_ref)]
        tiles.append(jnp.concatenate(parts, axis=0))
    return jnp.concatenate(tiles, axis=1)


def project(token_refs, near_ref, far_ref):
    total = None
    x, y = lax.axis_index("col") // 4, lax.axis_index("row") // 2
    for step, token_ref in enumerate(token_refs):
        moved = lax.rem(2 * x + step + 4 - y, 4)
        part = dot_f32(token_ref[...], step_weight(moved, near_ref, far_ref))
        total = part if total is None else total + part
    return total.astype(BF16)


def own_states(column, packet_refs):
    total = jnp.zeros((2 * HD, HD), F32)
    for packet_ref in packet_refs:
        for step in range(4):
            for place in range(2):
                mark = packet_ref[step, place, MARK : MARK + 16, :].astype(F32)[0:1]
                state = packet_ref[step, place, STATE : STATE + 2 * HD, :].astype(F32)
                total = total + jnp.where(mark == column, state, 0.0)
    return total[:HD], total[HD:]


def prefill(
    first, count, projected, persist_key, persist_value, memory, momentum, rates, out_ref, out_at
):
    forget_ref, keep_ref, learn_ref = rates
    blank = jnp.zeros((HD - MCH - PERS, HD), BF16)
    row_at = lax.broadcasted_iota(jnp.int32, (MCH, HD), 0)
    column_at = lax.broadcasted_iota(jnp.int32, (MCH, HD), 1)
    visible = (column_at <= row_at) | ((column_at >= MCH) & (column_at < MCH + PERS))
    for step in range(count):
        block = first + step
        here = slice(step * MCH, step * MCH + MCH)
        query = projected[here, 0:HD]
        key = projected[here, HD : 2 * HD]
        value = projected[here, 2 * HD : 3 * HD]
        query_scale = inverse_norm(query)
        key_scale = inverse_norm(key)
        left = jnp.concatenate(
            [jnp.concatenate([query, query], axis=1), jnp.concatenate([key, key], axis=1)], axis=0
        )
        reads = dot_f32(left, two_parts(memory))
        errors = reads[MCH:] * key_scale - value.astype(F32)
        errors = errors * (key_scale * (2.0 / MCH))
        gradient = dot_turned(jnp.concatenate([key, key], axis=0), two_parts(errors))
        momentum = keep_ref[block] * momentum - learn_ref[block] * gradient
        memory = (1.0 - forget_ref[block]) * memory + momentum

        keys = jnp.concatenate([key, persist_key, blank], axis=0)
        values = jnp.concatenate([value, persist_value, blank], axis=0)
        scores = jnp.where(visible, dot_rows(query, keys) * SCALE, -jnp.inf)
        powers = jnp.exp(scores - jnp.max(scores, axis=-1, keepdims=True))
        weights = (powers / jnp.sum(powers, axis=-1, keepdims=True)).astype(BF16)
        result = dot_f32(weights, values) + reads[:MCH] * query_scale
        out_ref[out_at + step * MCH : out_at + step * MCH + MCH, :] = result.astype(BF16)
    return memory, momentum


def decode(
    whole_ref, projected, persist_key, persist_value, decode_memory_ref, cache, score
):
    query = projected[HALF : HALF + EXTRA, 0:HD]
    key = projected[HALF : HALF + EXTRA, HD : 2 * HD]
    value = projected[HALF : HALF + EXTRA, 2 * HD : 3 * HD]
    row = lax.broadcasted_iota(jnp.int32, (EXTRA, 1), 0)
    length = jnp.zeros((EXTRA, 1), jnp.int32)
    for request in range(DEC_DEV):
        length = jnp.where(row == request, whole_ref[DEC_DEV * PAGES + request], length)
    for place in range(PAGES):
        span = slice(place * 2 * PAGE, place * 2 * PAGE + 2 * PAGE)
        found = dot_rows(query, cache[0, span, :])
        for request in range(1, DEC_DEV):
            found = jnp.where(row == request, dot_rows(query, cache[request, span, :]), found)
        column = lax.broadcasted_iota(jnp.int32, (EXTRA, 2 * PAGE), 1)
        live = ((column & 1) == 0) & ((column >> 1) + place * PAGE < length)
        score[:, span] = jnp.where(live, found * SCALE, -jnp.inf)
    own_score = jnp.sum(query.astype(F32) * key.astype(F32), axis=-1, keepdims=True) * SCALE
    persist_score = dot_rows(query, persist_key) * SCALE
    cache_score = score[...]
    largest = jnp.maximum(
        jnp.maximum(jnp.max(cache_score, axis=-1, keepdims=True), own_score),
        jnp.max(persist_score, axis=-1, keepdims=True),
    )
    cache_power = jnp.exp(cache_score - largest)
    own_power = jnp.exp(own_score - largest)
    persist_power = jnp.exp(persist_score - largest)
    totals = (
        jnp.sum(cache_power, axis=-1, keepdims=True)
        + own_power
        + jnp.sum(persist_power, axis=-1, keepdims=True)
    )
    share = 1.0 / totals
    cache_weight = pltpu.roll(cache_power * share, 1, 1).astype(BF16)
    attended = jnp.zeros((EXTRA, HD), F32)
    for request in range(DEC_DEV):
        attended = jnp.where(row == request, dot_f32(cache_weight, cache[request]), attended)
    own_weight = (own_power * share).astype(BF16).astype(F32)
    attended = attended + own_weight * value.astype(F32)
    attended = attended + dot_f32((persist_power * share).astype(BF16), persist_value)
    twice = jnp.concatenate([query, query], axis=1)
    readout = jnp.zeros((EXTRA, HD), F32)
    for request in range(DEC_DEV):
        read = dot_f32(twice, decode_memory_ref[request])
        readout = jnp.where(row == request, read, readout)
    return (attended + readout * inverse_norm(query)).astype(BF16)


class Rate:
    def __init__(self, rates_ref, kind):
        self.rates_ref, self.start = rates_ref, kind * (PCH // MCH)

    def __getitem__(self, block):
        return self.rates_ref[self.start + block]


def first_kernel(*refs):
    token_refs, packet_refs = refs[0:4], refs[4:6]
    whole_ref, rates_ref, persist_ref, decode_memory_ref, cache = refs[6:11]
    out_ref, tail_ref, memory_ref, momentum_ref = refs[11:15]
    projected, score = refs[15:]
    projected[...] = project(token_refs, *packet_refs)
    memory, momentum = own_states(lax.axis_index("col").astype(F32), packet_refs)
    persist_key, persist_value = persist_ref[0:PERS, :], persist_ref[PERS:, :]
    rates = [Rate(rates_ref, kind) for kind in range(3)]
    memory, momentum = prefill(
        0, HALF // MCH, projected, persist_key, persist_value, memory, momentum, rates, out_ref, 0
    )
    memory_ref[...] = memory
    momentum_ref[...] = momentum
    tail_ref[...] = decode(
        whole_ref, projected, persist_key, persist_value, decode_memory_ref, cache, score
    )


def second_kernel(*refs):
    token_refs, packet_refs, rates_ref, persist_ref = refs[0:4], refs[4:6], refs[6], refs[7]
    memory_in_ref, momentum_in_ref, first_ref, tail_ref = refs[8:12]
    out_ref, memory_ref, momentum_ref, projected = refs[12:]
    projected[...] = project(token_refs, *packet_refs)
    memory, momentum = prefill(
        HALF // MCH,
        REST // MCH,
        projected,
        persist_ref[0:PERS, :],
        persist_ref[PERS:, :],
        memory_in_ref[...],
        momentum_in_ref[...],
        [Rate(rates_ref, kind) for kind in range(3)],
        out_ref,
        HALF,
    )
    memory_ref[...] = memory
    momentum_ref[...] = momentum
    out_ref[0:HALF, :] = first_ref[...]
    out_ref[PCH:ROWS, :] = tail_ref[0:DEC_DEV, :]


IN_SMEM = pl.BlockSpec(memory_space=pltpu.SMEM)
IN_VMEM = pl.BlockSpec(memory_space=pltpu.VMEM)


IN_HBM = pl.BlockSpec(memory_space=pltpu.HBM)


def page_kernel(whole_ref, page_ref, cache_ref, arrival):
    for request in range(DEC_DEV):
        for place in range(PAGES):
            pltpu.make_async_copy(
                page_ref.at[whole_ref[request * PAGES + place]],
                cache_ref.at[request, pl.ds(place * 2 * PAGE, 2 * PAGE)],
                arrival.at[request],
            ).start()
    for request in range(DEC_DEV):
        whole = cache_ref.at[request]
        pltpu.make_async_copy(whole, whole, arrival.at[request]).wait()


def order_pages(whole, pages):
    return pl.pallas_call(
        page_kernel,
        out_shape=jax.ShapeDtypeStruct((DEC_DEV, 2 * CACHE, HD), BF16),
        in_specs=[IN_SMEM, IN_HBM],
        out_specs=IN_VMEM,
        scratch_shapes=[pltpu.SemaphoreType.DMA((DEC_DEV,))],
        compiler_params=pltpu.CompilerParams(vmem_limit_bytes=42 * 2**20),
    )(whole, pages.reshape(DEC_DEV * PAGES, 2 * PAGE, HD))


def first_part(whole, rates, chunks, packets, persist, decode_memory, cache):
    return pl.pallas_call(
        first_kernel,
        out_shape=(
            jax.ShapeDtypeStruct((HALF, HD), BF16),
            jax.ShapeDtypeStruct((EXTRA, HD), BF16),
            jax.ShapeDtypeStruct((HD, HD), F32),
            jax.ShapeDtypeStruct((HD, HD), F32),
        ),
        in_specs=[IN_VMEM] * 6 + [IN_SMEM] * 2 + [IN_VMEM] * 3,
        out_specs=(IN_VMEM,) * 4,
        scratch_shapes=[
            pltpu.VMEM((HALF + EXTRA, 3 * HD), BF16),
            pltpu.VMEM((EXTRA, 2 * CACHE), F32),
        ],
        compiler_params=pltpu.CompilerParams(vmem_limit_bytes=16 * 2**20),
    )(
        *chunks,
        *packets,
        whole,
        rates,
        persist,
        decode_memory,
        cache,
    )


def second_part(rates, chunks, packets, persist, memory, momentum, first, tail):
    return pl.pallas_call(
        second_kernel,
        out_shape=(
            jax.ShapeDtypeStruct((ROWS, HD), BF16),
            jax.ShapeDtypeStruct((HD, HD), F32),
            jax.ShapeDtypeStruct((HD, HD), F32),
        ),
        in_specs=[IN_VMEM] * 6 + [IN_SMEM] + [IN_VMEM] * 5,
        out_specs=(IN_VMEM,) * 3,
        scratch_shapes=[pltpu.VMEM((REST, 3 * HD), BF16)],
        compiler_params=pltpu.CompilerParams(vmem_limit_bytes=16 * 2**20),
    )(*chunks, *packets, rates, persist, memory, momentum, first, tail)


def pair_up(piece):
    other = permute(piece, lambda x, y, z_hi, z_lo, core: (x, y, 1 - z_hi, z_lo, core))
    return jnp.concatenate([piece, other], axis=1)


def spread_rows(pair):
    came = [
        permute(
            pair,
            lambda x, y, z_hi, z_lo, core, step=step: (x, (y + step) % 4, z_hi, z_lo, core),
        )
        for step in (1, 2, 3)
    ]
    return [pair, *came]


def packet_kernel(destination_ref, weight_ref, memory_ref, momentum_ref, packet_ref):
    for tile in range(3):
        packet_ref[tile * MCH : tile * MCH + MCH, :] = weight_ref[:, tile * HD : tile * HD + HD]
    states = jnp.concatenate([memory_ref[...], momentum_ref[...]], axis=0)
    high = states.astype(BF16)
    packet_ref[STATE : STATE + 2 * HD, :] = high
    packet_ref[MARK:PACKET, :] = jnp.full((16, HD), destination_ref[0].astype(F32)).astype(BF16)


def make_packet(weight, memory_in, momentum_in, destination):
    return pl.pallas_call(
        packet_kernel,
        out_shape=jax.ShapeDtypeStruct((PACKET, HD), BF16),
        in_specs=[IN_SMEM] + [IN_VMEM] * 3,
        out_specs=IN_VMEM,
    )(destination, weight, memory_in.reshape(HD, HD), momentum_in.reshape(HD, HD))


def gather_packets(packet, turned, cache):
    same = lax.axis_index("row") % 2 == lax.axis_index("col") // 2 % 2
    other = permute(packet, lambda x, y, z_hi, z_lo, core: (x, y, z_hi, 1 - z_lo, core))
    other, turned, cache = lax.optimization_barrier((other, turned, cache))
    pair = jnp.stack([jnp.where(same, packet, other), jnp.where(same, other, packet)], axis=0)
    near = [pair]
    for step in (1, 2, 3):
        near.append(
            permute(
                pair,
                lambda x, y, z_hi, z_lo, core, step=step: ((x + step) % 4, y, z_hi, z_lo, core),
            )
        )
    return near, turned, cache


def exchange_packets(near, after):
    near[3], _ = lax.optimization_barrier((near[3], after))
    near = jnp.stack(near, axis=0)
    far = permute(near, lambda x, y, z_hi, z_lo, core: (x, y, z_hi, z_lo, 1 - core))
    return near, far


def shards(
    tokens,
    qkv_weight,
    persistent,
    cache_pages,
    page_table,
    cache_len,
    destination,
    memory_in,
    momentum_in,
    forget_rate,
    keep_rate,
    learn_rate,
    decode_memory,
):
    core = lax.axis_index("col") % 2
    lower, upper = tokens[:ROWS], tokens[ROWS:]
    kept = jnp.where(core == 0, lower, upper)
    sent = jnp.where(core == 0, upper, lower)
    came = permute(sent, lambda x, y, z_hi, z_lo, core: (x, y, z_hi, z_lo, 1 - core))
    own = jnp.concatenate([kept, came], axis=1)
    (
        own,
        persistent,
        page_table,
        cache_len,
        forget_rate,
        keep_rate,
        learn_rate,
        decode_memory,
    ) = lax.optimization_barrier(
        (
            own,
            persistent,
            page_table,
            cache_len,
            forget_rate,
            keep_rate,
            learn_rate,
            decode_memory,
        )
    )
    parts = [
        jnp.concatenate([own[:HALF], jnp.pad(own[PCH:], ((0, PADDED - ROWS), (0, 0)))], axis=0),
        own[HALF:PCH],
    ]
    turned = permute(
        jnp.concatenate(parts, axis=0),
        lambda x, y, z_hi, z_lo, core: (y, (x + y) % 4, z_lo, z_hi, core),
    )
    whole = jnp.concatenate([page_table.reshape(-1), cache_len], axis=0)
    cache = order_pages(whole, cache_pages)
    packet = make_packet(qkv_weight, memory_in, momentum_in, destination)
    packets, turned, cache = gather_packets(packet, turned, cache)
    pair = pair_up(turned)
    pairs = [pair[: HALF + EXTRA], pair[HALF + EXTRA :]]
    chunks = [spread_rows(pair) for pair in pairs]
    packets = exchange_packets(packets, [chunks[0][1], chunks[0][2], chunks[0][3]])
    rates = jnp.concatenate(
        [rate.reshape(-1) for rate in (forget_rate, keep_rate, learn_rate)], axis=0
    )
    persist = jnp.concatenate([persistent[:, 0], persistent[:, 1]], axis=0)
    decode_memory = decode_memory.reshape(DEC_DEV, HD, HD)
    high = decode_memory.astype(BF16)
    decode_parts = jnp.concatenate(
        [high, (decode_memory - high.astype(F32)).astype(BF16)], axis=1
    )
    first, tail, memory, momentum = first_part(
        whole,
        rates,
        chunks[0],
        packets,
        persist,
        decode_parts,
        cache,
    )
    heads_out, memory, momentum = second_part(
        rates, chunks[1], packets, persist, memory, momentum, first, tail
    )
    return heads_out, memory[None, None], momentum[None, None]


def solution(mesh):
    placed = (
        P("row", "col"),
        P("col", "row"),
        P(None, None, "row"),
        P("col", None, None, "row"),
        P("col", None),
        P("col"),
        P("col"),
        P("col", "row", None, None),
        P("col", "row", None, None),
        P("col", "row", None),
        P("col", "row", None),
        P("col", "row", None),
        P("col", "row", None, None),
    )
    return jax.shard_map(
        shards,
        mesh=mesh,
        in_specs=placed,
        out_specs=(P("col", "row"), P("col", "row", None, None), P("col", "row", None, None)),
        check_vma=False,
    )
```

```python
import jax
import jax.numpy as jnp
from jax import lax
from jax.experimental import pallas as pl
from jax.experimental.pallas import tpu as pltpu
from jax.sharding import PartitionSpec as P

HD = 128
PERS = 16
MCH = 64
PCH = 1024
DEC_DEV = 4
CACHE = 4096
PAGE = 256
PAGES = CACHE // PAGE
ROWS = PCH + DEC_DEV
PADDED = PCH + 16

F32 = jnp.float32
BF16 = jnp.bfloat16
EPSILON = 1e-6
SCALE = HD**-0.5


def device_at(x, y, z_hi, z_lo, core):
    return (2 * y + z_hi) * 16 + 4 * x + 2 * z_lo + core


def moves(target):
    pairs = []
    for x in range(4):
        for y in range(4):
            for z_hi in range(2):
                for z_lo in range(2):
                    for core in range(2):
                        here = (x, y, z_hi, z_lo, core)
                        pairs.append((device_at(*here), device_at(*target(*here))))
    return pairs


def permute(values, target):
    return lax.ppermute(values, ("row", "col"), moves(target))


def dot_f32(left, right):
    return lax.dot_general(left, right, (((1,), (0,)), ((), ())), preferred_element_type=F32)


def dot_rows(left, right):
    return lax.dot_general(left, right, (((1,), (1,)), ((), ())), preferred_element_type=F32)


def dot_turned(left, right):
    return lax.dot_general(left, right, (((0,), (0,)), ((), ())), preferred_element_type=F32)


def two_parts(values):
    high = values.astype(BF16)
    return jnp.concatenate([high, (values - high.astype(F32)).astype(BF16)], axis=0)


def inverse_norm(rows):
    wide = rows.astype(F32)
    return lax.rsqrt(jnp.sum(wide * wide, axis=-1, keepdims=True) + EPSILON)


HALF = 704
REST = PCH - HALF
EXTRA = PADDED - PCH
STATE = 3 * MCH
MARK = STATE + 2 * HD
PACKET = MARK + 16


def step_weight(step, near_ref, far_ref):
    tiles = []
    for tile in range(3):
        rows = slice(tile * MCH, tile * MCH + MCH)
        parts = [ref[step, place, rows, :] for place in range(2) for ref in (near_ref, far_ref)]
        tiles.append(jnp.concatenate(parts, axis=0))
    return jnp.concatenate(tiles, axis=1)


def project(token_refs, near_ref, far_ref):
    total = None
    x, y = lax.axis_index("col") // 4, lax.axis_index("row") // 2
    for step, token_ref in enumerate(token_refs):
        moved = lax.rem(2 * x + step + 4 - y, 4)
        part = dot_f32(token_ref[...], step_weight(moved, near_ref, far_ref))
        total = part if total is None else total + part
    return total.astype(BF16)


def own_states(column, packet_refs):
    total = jnp.zeros((2 * HD, HD), F32)
    for packet_ref in packet_refs:
        for step in range(4):
            for place in range(2):
                mark = packet_ref[step, place, MARK : MARK + 16, :].astype(F32)[0:1]
                state = packet_ref[step, place, STATE : STATE + 2 * HD, :].astype(F32)
                total = total + jnp.where(mark == column, state, 0.0)
    return total[:HD], total[HD:]


def prefill(
    first, count, projected, persist_key, persist_value, memory, momentum, rates, out_ref, out_at
):
    forget_ref, keep_ref, learn_ref = rates
    blank = jnp.zeros((HD - MCH - PERS, HD), BF16)
    row_at = lax.broadcasted_iota(jnp.int32, (MCH, HD), 0)
    column_at = lax.broadcasted_iota(jnp.int32, (MCH, HD), 1)
    visible = (column_at <= row_at) | ((column_at >= MCH) & (column_at < MCH + PERS))
    for step in range(count):
        block = first + step
        here = slice(step * MCH, step * MCH + MCH)
        query = projected[here, 0:HD]
        key = projected[here, HD : 2 * HD]
        value = projected[here, 2 * HD : 3 * HD]
        query_scale = inverse_norm(query)
        key_scale = inverse_norm(key)
        left = jnp.concatenate(
            [jnp.concatenate([query, query], axis=1), jnp.concatenate([key, key], axis=1)], axis=0
        )
        reads = dot_f32(left, two_parts(memory))
        errors = reads[MCH:] * key_scale - value.astype(F32)
        errors = errors * (key_scale * (2.0 / MCH))
        gradient = dot_turned(jnp.concatenate([key, key], axis=0), two_parts(errors))
        momentum = keep_ref[block] * momentum - learn_ref[block] * gradient
        memory = (1.0 - forget_ref[block]) * memory + momentum

        keys = jnp.concatenate([key, persist_key, blank], axis=0)
        values = jnp.concatenate([value, persist_value, blank], axis=0)
        scores = jnp.where(visible, dot_rows(query, keys) * SCALE, -jnp.inf)
        powers = jnp.exp(scores - jnp.max(scores, axis=-1, keepdims=True))
        weights = (powers / jnp.sum(powers, axis=-1, keepdims=True)).astype(BF16)
        result = dot_f32(weights, values) + reads[:MCH] * query_scale
        out_ref[out_at + step * MCH : out_at + step * MCH + MCH, :] = result.astype(BF16)
    return memory, momentum


def decode(
    whole_ref, projected, persist_key, persist_value, decode_memory_ref, cache, score
):
    query = projected[HALF : HALF + EXTRA, 0:HD]
    key = projected[HALF : HALF + EXTRA, HD : 2 * HD]
    value = projected[HALF : HALF + EXTRA, 2 * HD : 3 * HD]
    row = lax.broadcasted_iota(jnp.int32, (EXTRA, 1), 0)
    length = jnp.zeros((EXTRA, 1), jnp.int32)
    for request in range(DEC_DEV):
        length = jnp.where(row == request, whole_ref[DEC_DEV * PAGES + request], length)
    for place in range(PAGES):
        span = slice(place * 2 * PAGE, place * 2 * PAGE + 2 * PAGE)
        found = dot_rows(query, cache[0, span, :])
        for request in range(1, DEC_DEV):
            found = jnp.where(row == request, dot_rows(query, cache[request, span, :]), found)
        column = lax.broadcasted_iota(jnp.int32, (EXTRA, 2 * PAGE), 1)
        live = ((column & 1) == 0) & ((column >> 1) + place * PAGE < length)
        score[:, span] = jnp.where(live, found * SCALE, -jnp.inf)
    own_score = jnp.sum(query.astype(F32) * key.astype(F32), axis=-1, keepdims=True) * SCALE
    persist_score = dot_rows(query, persist_key) * SCALE
    cache_score = score[...]
    largest = jnp.maximum(
        jnp.maximum(jnp.max(cache_score, axis=-1, keepdims=True), own_score),
        jnp.max(persist_score, axis=-1, keepdims=True),
    )
    cache_power = jnp.exp(cache_score - largest)
    own_power = jnp.exp(own_score - largest)
    persist_power = jnp.exp(persist_score - largest)
    totals = (
        jnp.sum(cache_power, axis=-1, keepdims=True)
        + own_power
        + jnp.sum(persist_power, axis=-1, keepdims=True)
    )
    share = 1.0 / totals
    cache_weight = pltpu.roll(cache_power * share, 1, 1).astype(BF16)
    attended = jnp.zeros((EXTRA, HD), F32)
    for request in range(DEC_DEV):
        attended = jnp.where(row == request, dot_f32(cache_weight, cache[request]), attended)
    own_weight = (own_power * share).astype(BF16).astype(F32)
    attended = attended + own_weight * value.astype(F32)
    attended = attended + dot_f32((persist_power * share).astype(BF16), persist_value)
    twice = jnp.concatenate([query, query], axis=1)
    readout = jnp.zeros((EXTRA, HD), F32)
    for request in range(DEC_DEV):
        read = dot_f32(twice, decode_memory_ref[request])
        readout = jnp.where(row == request, read, readout)
    return (attended + readout * inverse_norm(query)).astype(BF16)


class Rate:
    def __init__(self, rates_ref, kind):
        self.rates_ref, self.start = rates_ref, kind * (PCH // MCH)

    def __getitem__(self, block):
        return self.rates_ref[self.start + block]


def first_kernel(*refs):
    token_refs, packet_refs = refs[0:4], refs[4:6]
    whole_ref, rates_ref, persist_ref, decode_memory_ref, cache = refs[6:11]
    out_ref, tail_ref, memory_ref, momentum_ref = refs[11:15]
    projected, score = refs[15:]
    projected[...] = project(token_refs, *packet_refs)
    memory, momentum = own_states(lax.axis_index("col").astype(F32), packet_refs)
    persist_key, persist_value = persist_ref[0:PERS, :], persist_ref[PERS:, :]
    rates = [Rate(rates_ref, kind) for kind in range(3)]
    memory, momentum = prefill(
        0, HALF // MCH, projected, persist_key, persist_value, memory, momentum, rates, out_ref, 0
    )
    memory_ref[...] = memory
    momentum_ref[...] = momentum
    tail_ref[...] = decode(
        whole_ref, projected, persist_key, persist_value, decode_memory_ref, cache, score
    )


def second_kernel(*refs):
    token_refs, packet_refs, rates_ref, persist_ref = refs[0:4], refs[4:6], refs[6], refs[7]
    memory_in_ref, momentum_in_ref, first_ref, tail_ref = refs[8:12]
    out_ref, memory_ref, momentum_ref, projected = refs[12:]
    projected[...] = project(token_refs, *packet_refs)
    memory, momentum = prefill(
        HALF // MCH,
        REST // MCH,
        projected,
        persist_ref[0:PERS, :],
        persist_ref[PERS:, :],
        memory_in_ref[...],
        momentum_in_ref[...],
        [Rate(rates_ref, kind) for kind in range(3)],
        out_ref,
        HALF,
    )
    memory_ref[...] = memory
    momentum_ref[...] = momentum
    out_ref[0:HALF, :] = first_ref[...]
    out_ref[PCH:ROWS, :] = tail_ref[0:DEC_DEV, :]


IN_SMEM = pl.BlockSpec(memory_space=pltpu.SMEM)
IN_VMEM = pl.BlockSpec(memory_space=pltpu.VMEM)


IN_HBM = pl.BlockSpec(memory_space=pltpu.HBM)


def page_kernel(whole_ref, page_ref, cache_ref, arrival):
    for request in range(DEC_DEV):
        for place in range(PAGES):
            pltpu.make_async_copy(
                page_ref.at[whole_ref[request * PAGES + place]],
                cache_ref.at[request, pl.ds(place * 2 * PAGE, 2 * PAGE)],
                arrival.at[request],
            ).start()
    for request in range(DEC_DEV):
        whole = cache_ref.at[request]
        pltpu.make_async_copy(whole, whole, arrival.at[request]).wait()


def order_pages(whole, pages):
    return pl.pallas_call(
        page_kernel,
        out_shape=jax.ShapeDtypeStruct((DEC_DEV, 2 * CACHE, HD), BF16),
        in_specs=[IN_SMEM, IN_HBM],
        out_specs=IN_VMEM,
        scratch_shapes=[pltpu.SemaphoreType.DMA((DEC_DEV,))],
        compiler_params=pltpu.CompilerParams(vmem_limit_bytes=42 * 2**20),
    )(whole, pages.reshape(DEC_DEV * PAGES, 2 * PAGE, HD))


def first_part(whole, rates, chunks, packets, persist, decode_memory, cache):
    return pl.pallas_call(
        first_kernel,
        out_shape=(
            jax.ShapeDtypeStruct((HALF, HD), BF16),
            jax.ShapeDtypeStruct((EXTRA, HD), BF16),
            jax.ShapeDtypeStruct((HD, HD), F32),
            jax.ShapeDtypeStruct((HD, HD), F32),
        ),
        in_specs=[IN_VMEM] * 6 + [IN_SMEM] * 2 + [IN_VMEM] * 3,
        out_specs=(IN_VMEM,) * 4,
        scratch_shapes=[
            pltpu.VMEM((HALF + EXTRA, 3 * HD), BF16),
            pltpu.VMEM((EXTRA, 2 * CACHE), F32),
        ],
        compiler_params=pltpu.CompilerParams(vmem_limit_bytes=16 * 2**20),
    )(
        *chunks,
        *packets,
        whole,
        rates,
        persist,
        decode_memory,
        cache,
    )


def second_part(rates, chunks, packets, persist, memory, momentum, first, tail):
    return pl.pallas_call(
        second_kernel,
        out_shape=(
            jax.ShapeDtypeStruct((ROWS, HD), BF16),
            jax.ShapeDtypeStruct((HD, HD), F32),
            jax.ShapeDtypeStruct((HD, HD), F32),
        ),
        in_specs=[IN_VMEM] * 6 + [IN_SMEM] + [IN_VMEM] * 5,
        out_specs=(IN_VMEM,) * 3,
        scratch_shapes=[pltpu.VMEM((REST, 3 * HD), BF16)],
        compiler_params=pltpu.CompilerParams(vmem_limit_bytes=16 * 2**20),
    )(*chunks, *packets, rates, persist, memory, momentum, first, tail)


def pair_up(piece):
    other = permute(piece, lambda x, y, z_hi, z_lo, core: (x, y, 1 - z_hi, z_lo, core))
    return jnp.concatenate([piece, other], axis=1)


def spread_rows(pair):
    came = [
        permute(
            pair,
            lambda x, y, z_hi, z_lo, core, step=step: (x, (y + step) % 4, z_hi, z_lo, core),
        )
        for step in (1, 2, 3)
    ]
    return [pair, *came]


def packet_kernel(destination_ref, weight_ref, memory_ref, momentum_ref, packet_ref):
    for tile in range(3):
        packet_ref[tile * MCH : tile * MCH + MCH, :] = weight_ref[:, tile * HD : tile * HD + HD]
    states = jnp.concatenate([memory_ref[...], momentum_ref[...]], axis=0)
    high = states.astype(BF16)
    packet_ref[STATE : STATE + 2 * HD, :] = high
    packet_ref[MARK:PACKET, :] = jnp.full((16, HD), destination_ref[0].astype(F32)).astype(BF16)


def make_packet(weight, memory_in, momentum_in, destination):
    return pl.pallas_call(
        packet_kernel,
        out_shape=jax.ShapeDtypeStruct((PACKET, HD), BF16),
        in_specs=[IN_SMEM] + [IN_VMEM] * 3,
        out_specs=IN_VMEM,
    )(destination, weight, memory_in.reshape(HD, HD), momentum_in.reshape(HD, HD))


def gather_packets(packet, turned, cache):
    same = lax.axis_index("row") % 2 == lax.axis_index("col") // 2 % 2
    other = permute(packet, lambda x, y, z_hi, z_lo, core: (x, y, z_hi, 1 - z_lo, core))
    other, turned, cache = lax.optimization_barrier((other, turned, cache))
    pair = jnp.stack([jnp.where(same, packet, other), jnp.where(same, other, packet)], axis=0)
    near = [pair]
    for step in (1, 2, 3):
        near.append(
            permute(
                pair,
                lambda x, y, z_hi, z_lo, core, step=step: ((x + step) % 4, y, z_hi, z_lo, core),
            )
        )
    return near, turned, cache


def exchange_packets(near, after):
    near[3], _ = lax.optimization_barrier((near[3], after))
    near = jnp.stack(near, axis=0)
    far = permute(near, lambda x, y, z_hi, z_lo, core: (x, y, z_hi, z_lo, 1 - core))
    return near, far


def shards(
    tokens,
    qkv_weight,
    persistent,
    cache_pages,
    page_table,
    cache_len,
    destination,
    memory_in,
    momentum_in,
    forget_rate,
    keep_rate,
    learn_rate,
    decode_memory,
):
    core = lax.axis_index("col") % 2
    lower, upper = tokens[:ROWS], tokens[ROWS:]
    kept = jnp.where(core == 0, lower, upper)
    sent = jnp.where(core == 0, upper, lower)
    came = permute(sent, lambda x, y, z_hi, z_lo, core: (x, y, z_hi, z_lo, 1 - core))
    own = jnp.concatenate([kept, came], axis=1)
    (
        own,
        persistent,
        page_table,
        cache_len,
        forget_rate,
        keep_rate,
        learn_rate,
        decode_memory,
    ) = lax.optimization_barrier(
        (
            own,
            persistent,
            page_table,
            cache_len,
            forget_rate,
            keep_rate,
            learn_rate,
            decode_memory,
        )
    )
    parts = [
        jnp.concatenate([own[:HALF], jnp.pad(own[PCH:], ((0, PADDED - ROWS), (0, 0)))], axis=0),
        own[HALF:PCH],
    ]
    turned = permute(
        jnp.concatenate(parts, axis=0),
        lambda x, y, z_hi, z_lo, core: (y, (x + y) % 4, z_lo, z_hi, core),
    )
    whole = jnp.concatenate([page_table.reshape(-1), cache_len], axis=0)
    cache = order_pages(whole, cache_pages)
    packet = make_packet(qkv_weight, memory_in, momentum_in, destination)
    packets, turned, cache = gather_packets(packet, turned, cache)
    pair = pair_up(turned)
    pairs = [pair[: HALF + EXTRA], pair[HALF + EXTRA :]]
    chunks = [spread_rows(pair) for pair in pairs]
    packets = exchange_packets(packets, [chunks[0][1], chunks[0][2], chunks[0][3]])
    rates = jnp.concatenate(
        [rate.reshape(-1) for rate in (forget_rate, keep_rate, learn_rate)], axis=0
    )
    persist = jnp.concatenate([persistent[:, 0], persistent[:, 1]], axis=0)
    decode_memory = decode_memory.reshape(DEC_DEV, HD, HD)
    high = decode_memory.astype(BF16)
    decode_parts = jnp.concatenate(
        [high, (decode_memory - high.astype(F32)).astype(BF16)], axis=1
    )
    first, tail, memory, momentum = first_part(
        whole,
        rates,
        chunks[0],
        packets,
        persist,
        decode_parts,
        cache,
    )
    heads_out, memory, momentum = second_part(
        rates, chunks[1], packets, persist, memory, momentum, first, tail
    )
    return heads_out, memory[None, None], momentum[None, None]


def solution(mesh):
    placed = (
        P("row", "col"),
        P("col", "row"),
        P(None, None, "row"),
        P("col", None, None, "row"),
        P("col", None),
        P("col"),
        P("col"),
        P("col", "row", None, None),
        P("col", "row", None, None),
        P("col", "row", None),
        P("col", "row", None),
        P("col", "row", None),
        P("col", "row", None, None),
    )
    return jax.shard_map(
        shards,
        mesh=mesh,
        in_specs=placed,
        out_specs=(P("col", "row"), P("col", "row", None, None), P("col", "row", None, None)),
        check_vma=False,
    )
```
